128 devices in a mesh: dp: 64 (over x, y, z_hi, core), ctx: 2 (over z_lo).
Axes of the slice: x: 4, y: 4, z: 4 (z_hi: 2, z_lo: 2; z = z_hi * 2 + z_lo), core: 2. Of those that a mesh axis runs over, the one named last changes fastest.
Arguments:
- tokens: bfloat16 [128, 1024, 384], P('dp', 'ctx'), may hold values from -6 to 6
- segment_ids: int32 [128, 1024], P('dp', 'ctx'), may hold values from 0 to 766, as said below
- out_grad: bfloat16 [128, 1024, 384], P('dp', 'ctx'), may hold values from -6 to 6
- qkv_weight: bfloat16 [384, 1152], P('dp'), may hold values from -0.3125 to 0.3125
- query_bias: bfloat16 [384], P('dp'), may hold values from -3 to 3
- value_bias: bfloat16 [384], P('dp'), may hold values from -3 to 3
- proj_weight: bfloat16 [384, 384], P('dp'), may hold values from -1.25 to 1.25
- proj_bias: bfloat16 [384], P('dp'), may hold values from -3 to 3
- first_gain: bfloat16 [384], P('dp'), may hold values from 0.099609375 to 1.8984375
- first_shift: bfloat16 [384], P('dp'), may hold values from -3 to 3
- up_weight: bfloat16 [384, 1536], P('dp'), may hold values from -0.3125 to 0.3125
- up_bias: bfloat16 [1536], P('dp'), may hold values from -3 to 3
- down_weight: bfloat16 [1536, 384], P('dp'), may hold values from -0.15625 to 0.15625
- down_bias: bfloat16 [384], P('dp'), may hold values from -3 to 3
- second_gain: bfloat16 [384], P('dp'), may hold values from 0.099609375 to 1.8984375
- second_shift: bfloat16 [384], P('dp'), may hold values from -3 to 3
Outputs:
- layer_out: bfloat16 [128, 1024, 384], P('dp', 'ctx')
- tokens_grad: bfloat16 [128, 1024, 384], P('dp', 'ctx')
- qkv_weight_grad: float32 [384, 1152], P('dp')
- query_bias_grad: float32 [384], P('dp')
- value_bias_grad: float32 [384], P('dp')
- proj_weight_grad: float32 [384, 384], P('dp')
- proj_bias_grad: float32 [384], P('dp')
- first_gain_grad: float32 [384], P('dp')
- first_shift_grad: float32 [384], P('dp')
- up_weight_grad: float32 [384, 1536], P('dp')
- up_bias_grad: float32 [1536], P('dp')
- down_weight_grad: float32 [1536, 384], P('dp')
- down_bias_grad: float32 [384], P('dp')
- second_gain_grad: float32 [384], P('dp')
- second_shift_grad: float32 [384], P('dp')
The draws below stay inside these ranges and needn't reach their ends.
Inputs may be any that keep to these rules, and one draw needn't show every extreme that they name: `segment_ids`: in each sequence the ids start at 0, never fall and rise by at most one from a position to the next; they rise only at positions 1 to 383 and 641 to 1023, so positions 384 to 640 lie in one document. In each aligned group of 16 sequences, one, drawn from the seed, is a single document of 1024 tokens, and the next one in the group (cyclically) rises at every position where a rise may fall, ending at 766.
All inputs are finite; a program needn't handle non-finite values.
Results may differ from the reference program's by a relative error of at most 0.02.
Values may be sent and summed in bfloat16 or wider, within the bound.
No kernel may reach another device: no remote copies, remote signals or barrier semaphores. Data moves between devices by JAX's collectives and lax.ppermute only.
A program may use at most 256 MiB of HBM per device.

```python
import math
import jax
import jax.numpy as jnp
from jax import lax

D = 384
HEADS = 12
HEAD_DIM = 32
FF = 1536
SEQ = 1024
SEQS = 128


def draw_segment_ids(key, part):
    key = jax.random.fold_in(key, 7)
    level_key, break_key, whole_key = jax.random.split(key, 3)
    block_count = SEQ // 32
    levels = jax.random.randint(level_key, (SEQS, block_count), 0, 5)
    rates = jnp.left_shift(jnp.ones_like(levels), levels)
    rates = jnp.repeat(rates, 32, axis=1)
    chosen = jax.random.randint(whole_key, (), 0, 16)
    single = jnp.arange(SEQS) % 16 == chosen
    dense = jnp.arange(SEQS) % 16 == (chosen + 1) % 16
    rates = jnp.where(single[:, None], 0, rates)
    rates = jnp.where(dense[:, None], 64, rates)
    rolled = jax.random.randint(break_key, (SEQS, SEQ), 0, 64)
    places = jnp.arange(SEQ)
    allowed = (places > 0) & ((places < SEQ // 2 - SEQ // 8) | (places > SEQ // 2 + SEQ // 8))
    breaks = jnp.where(allowed[None, :] & (rolled < rates), 1, 0).astype(jnp.int32)
    return jnp.cumsum(breaks, axis=1).astype(jnp.int32)


def block_levels(own_key, shape, shards, low, top_value):
    level, own = 1.0, jax.random.fold_in(own_key, 6)
    for axis_at, shards_of in shards:
        heights = jnp.exp(jax.random.uniform(jax.random.fold_in(own, axis_at), (shards_of,), jnp.float32, low / len(shards), top_value / len(shards)))
        level = level * jnp.repeat(heights, shape[axis_at] // shards_of).reshape([-1 if axis == axis_at else 1 for axis in range(len(shape))])
    return level


def scatter_about(rng, shape, spread, most, pieces=(), dtype=jnp.bfloat16):
    entries = spread * jax.random.normal(rng, shape, jnp.float32)
    if pieces:
        entries = entries * block_levels(rng, shape, pieces, -0.22, 0.18)
    return jnp.clip(entries, -most, most).astype(dtype)


def setup_inputs(seed: int = 0) -> dict:
    seeds = jax.random.split(jax.random.key(seed), 17)
    return {
        "tokens": scatter_about(seeds[0], (SEQS, SEQ, D), 1.0, 6.0, ((0, 64), (1, 2))),
        "segment_ids": draw_segment_ids(jax.random.fold_in(seeds[16], 71), 0),
        "out_grad": scatter_about(seeds[2], (SEQS, SEQ, D), 1.0, 6.0, ((0, 64), (1, 2))),
        "qkv_weight": scatter_about(seeds[3], (D, 3 * D), D ** -0.5, 0.3125, ((0, 64),)),
        "query_bias": scatter_about(seeds[4], (D,), 0.5, 3.0, ((0, 64),)),
        "value_bias": scatter_about(seeds[5], (D,), 0.5, 3.0, ((0, 64),)),
        "proj_weight": scatter_about(seeds[6], (D, D), (D // 16) ** -0.5, 1.25, ((0, 64),)),
        "proj_bias": scatter_about(seeds[7], (D,), 0.5, 3.0, ((0, 64),)),
        "first_gain": jnp.clip(1.0 + 0.18 * jax.random.normal(seeds[8], (D,), jnp.float32), 0.099609375, 1.8984375).astype(jnp.bfloat16),
        "first_shift": scatter_about(seeds[9], (D,), 0.5, 3.0, ((0, 64),)),
        "up_weight": scatter_about(seeds[10], (D, FF), D ** -0.5, 0.3125, ((0, 64),)),
        "up_bias": scatter_about(seeds[11], (FF,), 0.5, 3.0, ((0, 64),)),
        "down_weight": scatter_about(seeds[12], (FF, D), FF ** -0.5, 0.15625, ((0, 64),)),
        "down_bias": scatter_about(seeds[13], (D,), 0.5, 3.0, ((0, 64),)),
        "second_gain": jnp.clip(1.0 + 0.18 * jax.random.normal(seeds[14], (D,), jnp.float32), 0.099609375, 1.8984375).astype(jnp.bfloat16),
        "second_shift": scatter_about(seeds[15], (D,), 0.5, 3.0, ((0, 64),)),
    }


@jax.custom_vjp
def low(v):
    return lax.optimization_barrier(v.astype(jnp.bfloat16)).astype(jnp.float32)

@jax.custom_vjp
def low_back(v):
    return v

def low_keep(v):
    return (low(v), None)

def low_pass(kept, grad):
    return (grad,)

def back_keep(v):
    return (v, None)

def back_low(kept, grad):
    return (low(grad),)
low.defvjp(low_keep, low_pass)
low_back.defvjp(back_keep, back_low)
precise = lax.Precision.HIGHEST

def rounded_both(values_in):
    return low(low_back(values_in))

def layer_norm(hidden, gain_vec, shift_vec):
    row_mean = lax.optimization_barrier(jnp.mean(hidden, axis=-1, keepdims=True))
    centered = hidden - row_mean
    variance = lax.optimization_barrier(jnp.mean(centered * centered, axis=-1, keepdims=True))
    return centered * lax.rsqrt(variance + 1e-05) * gain_vec + shift_vec

def encoder_layer(params, inputs, doc_ids):
    qkv_weight, query_bias, value_bias, proj_weight, proj_bias, first_gain, first_shift, up_weight, up_bias, down_weight, down_bias, second_gain, second_shift = params
    seq_count = inputs.shape[0]
    seq_len = inputs.shape[1]
    model_width = inputs.shape[2]
    score_scale = 1.0 / math.sqrt(HEAD_DIM)
    packed = inputs.reshape(seq_count * seq_len, model_width)
    projected = jnp.dot(packed, qkv_weight, precision=precise)
    head_shape = (seq_count, seq_len, HEADS, HEAD_DIM)
    queries = rounded_both(projected[:, :model_width] + query_bias).reshape(head_shape)
    key_rows = rounded_both(projected[:, model_width:2 * model_width]).reshape(head_shape)
    values = rounded_both(projected[:, 2 * model_width:] + value_bias).reshape(head_shape)
    scores = low_back(jnp.einsum('aqhd,akhd->ahqk', queries, key_rows, precision=precise) * score_scale)
    same_doc = doc_ids[:, None, :, None] == doc_ids[:, None, None, :]
    scores = jnp.where(same_doc, scores, -1e+30)
    attn_probs = low(jax.nn.softmax(scores, axis=-1))
    mixed_heads = jnp.einsum('ahqk,akhd->aqhd', attn_probs, values, precision=precise)
    mixed_heads = rounded_both(mixed_heads.reshape(seq_count * seq_len, model_width))
    attn_out = low_back(jnp.dot(mixed_heads, proj_weight, precision=precise) + proj_bias)
    first_norm = layer_norm(packed + attn_out, first_gain, first_shift)
    up_act = low_back(jnp.dot(low(first_norm), up_weight, precision=precise) + up_bias)
    activated = low(jax.nn.gelu(up_act, approximate=False))
    branch = low_back(jnp.dot(activated, down_weight, precision=precise) + down_bias)
    result = layer_norm(first_norm + branch, second_gain, second_shift)
    return result.reshape(seq_count, seq_len, model_width)

def reference(tokens, segment_ids, out_grad, qkv_weight, query_bias, value_bias, proj_weight, proj_bias, first_gain, first_shift, up_weight, up_bias, down_weight, down_bias, second_gain, second_shift):
    params = (qkv_weight.astype(jnp.float32), query_bias.astype(jnp.float32), value_bias.astype(jnp.float32), proj_weight.astype(jnp.float32), proj_bias.astype(jnp.float32), first_gain.astype(jnp.float32), first_shift.astype(jnp.float32), up_weight.astype(jnp.float32), up_bias.astype(jnp.float32), down_weight.astype(jnp.float32), down_bias.astype(jnp.float32), second_gain.astype(jnp.float32), second_shift.astype(jnp.float32))
    group_size = math.gcd(SEQS, max(1, 4096 // SEQ))
    step_count = SEQS // group_size
    block_fn = jax.checkpoint(encoder_layer)
    grouped_ids = segment_ids.reshape(step_count, group_size, SEQ)

    def whole(weights, inputs):
        grouped = inputs.reshape(step_count, group_size, SEQ, D)

        def advance(carried, slice_pair):
            return (carried, block_fn(weights, slice_pair[0], slice_pair[1]))
        _, stacked = lax.scan(advance, jnp.float32(0.0), (grouped, grouped_ids))
        return stacked.reshape(SEQS, SEQ, D)
    result, pullback = jax.vjp(whole, params, tokens.astype(jnp.float32))
    param_grads, token_grad = pullback(out_grad.astype(jnp.float32))
    qkv_grad, query_bias_grad, value_bias_grad, proj_grad, proj_bias_grad, first_gain_grad, first_shift_grad, up_grad, up_bias_grad, down_grad, down_bias_grad, second_gain_grad, second_shift_grad = param_grads
    return (result.astype(jnp.bfloat16), token_grad.astype(jnp.bfloat16), qkv_grad, query_bias_grad, value_bias_grad, proj_grad, proj_bias_grad, first_gain_grad, first_shift_grad, up_grad, up_bias_grad, down_grad, down_bias_grad, second_gain_grad, second_shift_grad)
```

```python
import functools
import math

import jax
import jax.numpy as jnp
import numpy as np
from jax import lax
from jax.experimental import pallas as pl
from jax.experimental.pallas import tpu as pltpu
from jax.sharding import Mesh
from jax.sharding import PartitionSpec as P

D = 384
FF = 1536
SEQ = 1024
HALF = 512
PART = 192
RANKS = 64
ROWS = D // RANKS
SCALE = 1.0 / math.sqrt(32)
LOG2E = math.log2(math.e)
BOUND = 60.0

bf16 = jnp.bfloat16
f32 = jnp.float32
VMEM = pl.BlockSpec(memory_space=pltpu.VMEM)
SMEM = pl.BlockSpec(memory_space=pltpu.SMEM)
SWAP = ((0, 1), (1, 0))
ALL = ("g", "c", "zl")


def dot(left, right):
    return lax.dot_general(left, right, (((1,), (0,)), ((), ())), preferred_element_type=f32)


def dot_nt(left, right):
    return lax.dot_general(left, right, (((1,), (1,)), ((), ())), preferred_element_type=f32)


def dot_tn(left, right):
    return lax.dot_general(left, right, (((0,), (0,)), ((), ())), preferred_element_type=f32)


def joint_choice():
    choice = np.zeros((256, 256), np.float32)
    for rank in range(8):
        for block in range(5):
            for row in range(ROWS):
                choice[48 * block + ROWS * rank + row, 32 * rank + ROWS * block + row] = 1
        for place, row in ((240, 30), (241, 31), (242, 24), (243, 25)):
            choice[place, 32 * rank + row] = 1
    return choice


def rest_choice():
    choice = np.zeros((2, 448, 256), np.float32)
    for core in range(2):
        for at in range(4):
            rank = 2 * at + core
            for row in range(ROWS):
                for block in range(5):
                    choice[core, 48 * block + ROWS * rank + row, 64 * at + ROWS * block + row] = 1
            for row in range(24):
                choice[core, 240 + 24 * rank + row, 64 * at + 30 + row] = 1
            for row in range(10):
                choice[core, 432 + row, 64 * at + 54 + row] = 1
    return choice


def call(kernel, ins, outs, scratch=(), scalars=0, flops=0, name=None):
    return pl.pallas_call(
        kernel,
        in_specs=[SMEM] * scalars + [VMEM] * ins,
        out_specs=[VMEM] * len(outs),
        out_shape=[jax.ShapeDtypeStruct(shape, dtype) for shape, dtype in outs],
        scratch_shapes=scratch,
        compiler_params=pltpu.CompilerParams(vmem_limit_bytes=56 * 2**20),
        cost_estimate=pl.CostEstimate(flops=flops, bytes_accessed=4 * 2**20, transcendentals=0),
        name=name,
    )


def unpack_joint(packed, choice, weight, weight_t, bias, bias_t):
    low_lanes = lax.broadcasted_iota(jnp.int32, (48, 128), 1) < 64
    total = jnp.zeros((16, 128), f32)
    for step in range(8):
        out = dot(choice[...], packed[256 * step : 256 * step + 256, :])
        rows = slice(48 * step, 48 * step + 48)
        mixed = out[144:192]
        weight[rows, 0:128] = out[0:48].astype(bf16)
        weight[rows, 256:384] = out[48:96].astype(bf16)
        weight[rows, 512:640] = out[96:144].astype(bf16)
        weight[rows, 128:256] = jnp.where(low_lanes, mixed, 0.0).astype(bf16)
        weight[rows, 384:512] = jnp.where(low_lanes, pltpu.roll(mixed, 64, 1), 0.0).astype(bf16)
        weight[rows, 640:768] = jnp.where(low_lanes, out[192:240], 0.0).astype(bf16)
        total = total + out[240:256]
    tail = jnp.where(low_lanes[:16], pltpu.roll(total, 64, 1), 0.0)
    both = jnp.concatenate([total[0:2], jnp.zeros((6, 128), f32)], axis=0)
    tails = jnp.concatenate([tail[2:4], jnp.zeros((6, 128), f32)], axis=0)
    rows = jnp.concatenate([both, tails], axis=1)
    bias[...] = rows
    bias_t[...] = jnp.transpose(jnp.concatenate([rows, jnp.zeros((120, 256), f32)], axis=0))
    weight_t[...] = jnp.transpose(weight[...].astype(f32)).astype(bf16)


def padded_head(matrix, head, lanes, extra=None):
    parts = []
    if head:
        parts.append(jnp.zeros((32 * head, lanes), bf16))
    parts.append(matrix)
    if extra is None:
        parts.append(jnp.zeros((224 - 32 * head, lanes), bf16))
    else:
        if head < 5:
            parts.append(jnp.zeros((160 - 32 * head, lanes), bf16))
        parts.append(extra)
        parts.append(jnp.zeros((48, lanes), bf16))
    return jnp.concatenate(parts, axis=0)


def id_columns(id_row):
    return jnp.transpose(jnp.broadcast_to(id_row, (128, SEQ)))


def attend(place, own, received, weight, weight_t, bias, bias_t, id_row, q_rows, k_rows, v_rows, q_t, k_t, mixed_t, lse, v_t, ids_t):
    lane = lax.broadcasted_iota(jnp.int32, (HALF, 256), 1) < PART
    for half, block in ((place[0], own), (1 - place[0], received)):
        at = pl.ds(pl.multiple_of(half * HALF, HALF), HALF)
        tokens = block[...]
        flat = dot(tokens, weight[...])
        q_rows[at, :] = ((flat[:, 0:256] + bias[0:1, :]) * (SCALE * LOG2E)).astype(bf16)
        k_rows[at, :] = jnp.where(lane, flat[:, 256:512], 1.0).astype(bf16)
        v_rows[at, :] = jnp.where(lane, flat[:, 512:768] + bias[1:2, :], 1.0).astype(bf16)
        q_t[:, at] = ((dot_nt(weight_t[0:PART, :], tokens) + bias_t[0:PART, 0:1]) * (SCALE * LOG2E)).astype(bf16)
        k_t[:, at] = dot_nt(weight_t[256 : 256 + PART, :], tokens).astype(bf16)
        v_t[0:PART, at] = (dot_nt(weight_t[512 : 512 + PART, :], tokens) + bias_t[0:PART, 1:2]).astype(bf16)
    v_t[PART:, :] = jnp.ones((16, SEQ), bf16)
    ids_t[...] = id_columns(id_row[...])
    lse[...] = jnp.zeros_like(lse)
    largest = jnp.zeros((), f32)
    for head in range(6):
        rows = slice(32 * head, 32 * head + 32)
        q_size = jnp.max(jnp.sum(jnp.square(q_t[rows, :].astype(f32)), axis=0, keepdims=True))
        k_size = jnp.max(jnp.sum(jnp.square(k_t[rows, :].astype(f32)), axis=0, keepdims=True))
        largest = jnp.maximum(largest, q_size * k_size)

    def run(shift):
        def step(tile, carried):
            at = pl.ds(pl.multiple_of(tile * HALF, HALF), HALF)
            same = jnp.concatenate([ids_t[...]] * 4, axis=1) == id_row[:, at]
            keep = same.astype(f32).astype(bf16)
            for head in range(6):
                rows = slice(32 * head, 32 * head + 32)
                scores = dot(k_rows[...], padded_head(q_t[rows, at], head, HALF))
                if shift:
                    scores = jnp.where(same, scores, -1e30)
                    top = jnp.max(scores, axis=0, keepdims=True)
                    probs = jnp.exp2(scores - top).astype(bf16)
                else:
                    top = 0.0
                    probs = jnp.exp2(scores).astype(bf16) * keep
                mixed = dot(jnp.concatenate([v_t[rows, :], v_t[PART:, :]], axis=0), probs)
                total = mixed[32:33]
                mixed_t[rows, at] = (mixed[0:32] * (1.0 / total)).astype(bf16)
                lse[head : head + 1, at] = jnp.log2(total) + top
            return carried

        lax.fori_loop(0, SEQ // HALF, step, 0)

    @pl.when(largest <= BOUND * BOUND)
    def _():
        run(False)

    @pl.when(jnp.logical_not(largest <= BOUND * BOUND))
    def _():
        run(True)


def three_terms(row):
    first = row.astype(bf16).astype(f32)
    second = (row - first).astype(bf16).astype(f32)
    third = row - first - second
    return jnp.concatenate([first, second, third, jnp.zeros((13, row.shape[1]), f32)], axis=0).astype(bf16)


def attend_back(
    has_totals, place, own, received, weight_t, id_row, q_rows, k_rows, v_rows, q_t, k_t, mixed_t, lse, mixed_grad_t, *rest
):
    if has_totals:
        totals_in, bias_in, choice, tokens_grad, packed, q_grad_t, k_grad, v_grad, grad_rows, q_extra, o_extra, ids_t, x_rows = rest
    else:
        tokens_grad, totals_out, bias_out, q_grad_t, k_grad, v_grad, grad_rows, q_extra, o_extra, ids_t, x_rows = rest
    for half, block in ((place[0], own), (1 - place[0], received)):
        x_rows[pl.ds(pl.multiple_of(half * HALF, HALF), HALF), :] = block[...]
    ids_t[...] = id_columns(id_row[...])
    grad_rows[:, 0:PART] = jnp.transpose(mixed_grad_t[...].astype(f32)).astype(bf16)
    grad_rows[:, PART:] = jnp.zeros((SEQ, 256 - PART), bf16)
    for head in range(6):
        rows = slice(32 * head, 32 * head + 32)
        delta = jnp.sum(mixed_grad_t[rows, :].astype(f32) * mixed_t[rows, :].astype(f32), axis=0, keepdims=True)
        q_extra[16 * head : 16 * head + 16, :] = three_terms(-lse[head : head + 1, :])
        o_extra[16 * head : 16 * head + 16, :] = three_terms(-delta)
    q_grad_t[...] = jnp.zeros_like(q_grad_t)
    lane = lax.broadcasted_iota(jnp.int32, (SEQ, 256), 1)

    def step(tile, carried):
        at = pl.ds(pl.multiple_of(tile * 256, 256), 256)
        ids = ids_t[at, :]
        keep = (jnp.concatenate([ids] * 8, axis=1) == id_row[...]).astype(f32).astype(bf16)
        key_total = jnp.zeros((256, 256), f32)
        value_total = jnp.zeros((256, 256), f32)
        for head in range(6):
            rows = slice(32 * head, 32 * head + 32)
            extra = slice(16 * head, 16 * head + 16)
            inside = (lane >= 32 * head) & (lane < 32 * head + 32)
            scores = dot(k_rows[at, :], padded_head(q_t[rows, :], head, SEQ, q_extra[extra, :]))
            probs = jnp.exp2(jnp.minimum(scores, 1.0)).astype(bf16) * keep
            spread = dot(v_rows[at, :], padded_head(mixed_grad_t[rows, :], head, SEQ, o_extra[extra, :]))
            scores_grad = probs * spread.astype(bf16)
            key_total += dot(scores_grad, jnp.where(inside, q_rows[...], jnp.zeros_like(q_rows[...])))
            value_total += dot(probs, jnp.where(inside, grad_rows[...], jnp.zeros_like(grad_rows[...])))
            q_grad_t[rows, :] += dot(k_t[rows, at], scores_grad)
        k_grad[at, :] = (key_total * (1.0 / LOG2E)).astype(bf16)
        v_grad[at, :] = value_total.astype(bf16)
        return carried

    lax.fori_loop(0, SEQ // 256, step, 0)
    grad_rows[:, 0:PART] = jnp.transpose(q_grad_t[...] * SCALE).astype(bf16)
    tokens_grad[...] = (
        dot(grad_rows[:, 0:PART], weight_t[0:PART, :])
        + dot(k_grad[:, 0:PART], weight_t[256 : 256 + PART, :])
        + dot(v_grad[:, 0:PART], weight_t[512 : 512 + PART, :])
    ).astype(bf16)
    totals = [dot_tn(x_rows[...], part[...]) for part in (grad_rows, k_grad, v_grad)]
    bias_rows = jnp.concatenate(
        [jnp.sum(part[...].astype(f32), axis=0, keepdims=True) for part in (grad_rows, v_grad)]
        + [jnp.zeros((6, 256), f32)],
        axis=0,
    )
    if not has_totals:
        for at, part in enumerate(totals):
            totals_out[:, 256 * at : 256 * at + 256] = part
        bias_out[...] = bias_rows
        return
    q_all, k_all, v_all = (part + totals_in[:, 256 * at : 256 * at + 256] for at, part in enumerate(totals))
    bias_rows = bias_rows + bias_in[...]
    low_lanes = lax.broadcasted_iota(jnp.int32, (D, 128), 1) < 64
    fourth = jnp.where(low_lanes, q_all[:, 128:], pltpu.roll(k_all[:, 128:], 64, 1))
    fifth = jnp.where(low_lanes, v_all[:, 128:], 0.0)
    ends = jnp.where(low_lanes[:8], 0.0, pltpu.roll(bias_rows[:, 128:], 64, 1))
    biases = jnp.concatenate([bias_rows[0:2, 0:128], ends[0:2], jnp.zeros((12, 128), f32)], axis=0)
    for step_at in range(8):
        rows = slice(48 * step_at, 48 * step_at + 48)
        stacked = jnp.concatenate(
            [q_all[rows, 0:128], k_all[rows, 0:128], v_all[rows, 0:128], fourth[rows], fifth[rows], biases], axis=0
        ).astype(bf16)
        packed[256 * step_at : 256 * step_at + 256, :] = dot(choice[...], stacked).astype(bf16)


def normal_parts(values):
    mean = jnp.mean(values, axis=-1, keepdims=True)
    centered = values - mean
    scale = lax.rsqrt(jnp.mean(centered * centered, axis=-1, keepdims=True) + 1e-05)
    return centered * scale, scale


def normal_back(cotangent, normal, scale, gain):
    weighted = cotangent * gain
    mean = jnp.mean(weighted, axis=-1, keepdims=True)
    along = jnp.mean(weighted * normal, axis=-1, keepdims=True)
    return scale * (weighted - mean - normal * along)


def column_sum(matrix):
    return jnp.sum(matrix.astype(f32), axis=0, keepdims=True)


def feed_forward(
    place, own, received, own_grad, received_grad, mixed_a, mixed_b, packed_a, packed_b, choice, choice_t,
    out_own, out_received, attn_own, attn_received, back_a, back_b, packed_keep, packed_send,
    proj, up, down, up_total, down_total_t, proj_total, activated, slope,
):
    core, near = place[1], place[0]
    vectors = jnp.zeros((16, D), f32)
    for step in range(8):
        rows = slice(256 * step, 256 * step + 256)
        out = dot(choice[core], packed_a[rows, :]) + dot(choice[1 - core], packed_b[rows, :])
        proj[48 * step : 48 * step + 48, :] = out[0:48].astype(bf16)
        for block in range(4):
            up[48 * step : 48 * step + 48, D * block : D * block + D] = out[48 + 48 * block : 96 + 48 * block].astype(bf16)
        down[192 * step : 192 * step + 192, :] = out[240:432].astype(bf16)
        vectors = vectors + out[432:448]
    proj_bias, first_gain, first_shift, down_bias, second_gain, second_shift = (vectors[i : i + 1] for i in range(6))
    up_bias = jnp.concatenate([vectors[i : i + 1] for i in range(6, 10)], axis=1)
    rows_a = pl.ds(pl.multiple_of(core * PART, PART), PART)
    rows_b = pl.ds(pl.multiple_of((1 - core) * PART, PART), PART)
    sums = None
    for number, (half, block, grad_block, out_block, attn_block) in enumerate(
        ((near, own, own_grad, out_own, attn_own), (1 - near, received, received_grad, out_received, attn_received))
    ):
        at = pl.ds(pl.multiple_of(half * HALF, HALF), HALF)
        heads_a, heads_b = mixed_a[:, at], mixed_b[:, at]
        residual = block[...].astype(f32) + (dot_tn(heads_a, proj[rows_a, :]) + dot_tn(heads_b, proj[rows_b, :]) + proj_bias)
        first_normal, first_scale = normal_parts(residual)
        first_norm = first_normal * first_gain + first_shift
        first_low = first_norm.astype(bf16)
        for col in range(4):
            cols = slice(D * col, D * col + D)
            hidden = dot(first_low, up[:, cols]) + up_bias[:, cols]
            bell = jnp.exp2(hidden * hidden * (-0.5 * LOG2E))
            inner = 1.0 / (1.0 + jnp.abs(hidden) * (0.3275911 / math.sqrt(2)))
            series = inner * (0.127414796 + inner * (-0.142248368 + inner * (0.7107068705 + inner * (-0.7265760135 + inner * 0.5307027145))))
            tail = series * bell
            below = jnp.where(hidden >= 0.0, 1.0 - tail, tail)
            activated[:, cols] = (hidden * below).astype(bf16)
            slope[:, cols] = below + hidden * bell * (1.0 / math.sqrt(2 * math.pi))
        second_sum = first_norm + (dot(activated[...], down[...]) + down_bias)
        second_normal, second_scale = normal_parts(second_sum)
        out_block[...] = (second_normal * second_gain + second_shift).astype(bf16)
        out_grad = grad_block[...].astype(f32)
        second_grad = normal_back(out_grad, second_normal, second_scale, second_gain)
        branch_grad = second_grad.astype(bf16)
        first_grad = second_grad
        up_bias_grads = []
        for col in range(4):
            cols = slice(D * col, D * col + D)
            up_grad = (dot_nt(branch_grad, down[cols, :]) * slope[:, cols]).astype(bf16)
            first_grad = first_grad + dot_nt(up_grad, up[:, cols])
            up_bias_grads.append(column_sum(up_grad))
            up_new = dot_tn(first_low, up_grad)
            down_new = dot_tn(branch_grad, activated[:, cols])
            if number == 0:
                up_total[:, cols] = up_new
                down_total_t[:, cols] = down_new
            else:
                up_total[:, cols] += up_new
                down_total_t[:, cols] += down_new
        residual_grad = normal_back(first_grad, first_normal, first_scale, first_gain)
        attn_grad = residual_grad.astype(bf16)
        attn_block[...] = attn_grad
        back_a[:, at] = dot_nt(proj[rows_a, :], attn_grad).astype(bf16)
        back_b[:, at] = dot_nt(proj[rows_b, :], attn_grad).astype(bf16)
        new_a, new_b = dot(heads_a, attn_grad), dot(heads_b, attn_grad)
        if number == 0:
            proj_total[rows_a, :] = new_a
            proj_total[rows_b, :] = new_b
        else:
            proj_total[rows_a, :] += new_a
            proj_total[rows_b, :] += new_b
        new = [
            column_sum(attn_grad),
            column_sum(first_grad * first_normal),
            column_sum(first_grad),
            column_sum(branch_grad),
            column_sum(out_grad * second_normal),
            column_sum(out_grad),
        ] + up_bias_grads
        sums = new if sums is None else [a + b for a, b in zip(sums, new)]
    vector_rows = jnp.concatenate(sums + [jnp.zeros((6, D), f32)], axis=0)
    for pair in range(4):
        down_rows = jnp.transpose(down_total_t[:, D * pair : D * pair + D])
        for inner_step in range(2):
            step = 2 * pair + inner_step
            rows = slice(48 * step, 48 * step + 48)
            stacked = jnp.concatenate(
                [proj_total[rows, :]]
                + [up_total[rows, D * block : D * block + D] for block in range(4)]
                + [down_rows[192 * inner_step : 192 * inner_step + 192], vector_rows],
                axis=0,
            ).astype(bf16)
            packed_rows = slice(256 * step, 256 * step + 256)
            packed_keep[packed_rows, :] = dot(choice_t[core], stacked).astype(bf16)
            packed_send[packed_rows, :] = dot(choice_t[1 - core], stacked).astype(bf16)


def swap_core(value):
    return lax.ppermute(value, "c", SWAP)


def swap_ctx(value):
    return lax.ppermute(value, "zl", SWAP)


def spread_out(vector, rank):
    size = vector.shape[0]
    return lax.dynamic_update_slice(jnp.zeros((size * RANKS,), bf16), vector, (size * rank,))


def pack_joint(qkv_weight, query_bias, value_bias, rank):
    query_all, value_all = spread_out(query_bias, rank), spread_out(value_bias, rank)
    pieces = []
    for core in range(2):
        q, k, v = (qkv_weight[:, D * at + PART * core : D * at + PART * core + PART] for at in range(3))
        q_bias, v_bias = (part[PART * core : PART * core + PART] for part in (query_all, value_all))
        ends = jnp.concatenate([q_bias[None, 128:], v_bias[None, 128:], jnp.zeros((4, 64), bf16)], axis=0)
        pieces.append(
            jnp.concatenate(
                [
                    q[:, :128],
                    k[:, :128],
                    v[:, :128],
                    jnp.concatenate([q[:, 128:], k[:, 128:]], axis=1),
                    jnp.concatenate([v[:, 128:], ends], axis=1),
                    q_bias[None, :128],
                    v_bias[None, :128],
                ],
                axis=0,
            )
        )
    return jnp.stack(pieces)


def pack_rest(proj_weight, up_weight, down_weight, vectors, up_bias, rank):
    return jnp.concatenate(
        [proj_weight]
        + [up_weight[:, D * block : D * block + D] for block in range(4)]
        + [down_weight]
        + [spread_out(vector, rank)[None] for vector in vectors]
        + [spread_out(up_bias, rank).reshape(4, D)],
        axis=0,
    )


def local(
    tokens, segment_ids, out_grad, qkv_weight, query_bias, value_bias, proj_weight, proj_bias, first_gain, first_shift,
    up_weight, up_bias, down_weight, down_bias, second_gain, second_shift,
):
    group, core, near = (lax.axis_index(name) for name in ALL)
    rank = 2 * group + core
    groups = RANKS // 2
    place = jnp.stack([near, core]).astype(jnp.int32)
    take = functools.partial(lax.dynamic_index_in_dim, axis=0, keepdims=False)

    piece = pack_joint(qkv_weight, query_bias, value_bias, rank)
    piece = lax.dynamic_slice_in_dim(piece, 16 * near, 16, axis=1)
    sent = jnp.broadcast_to(piece[None, :, None], (groups, 2, 2, 16, 128)).reshape(4 * groups, 16, 128)
    joint_packed = lax.all_to_all(sent, ALL, 0, 0, tiled=True).reshape(groups * 64, 128)

    own = take(tokens, near)
    received = swap_ctx(take(tokens, 1 - near))
    ids_own = take(segment_ids, near)
    ids_received = swap_ctx(take(segment_ids, 1 - near))
    ids = jnp.where(near == 0, jnp.concatenate([ids_own, ids_received]), jnp.concatenate([ids_received, ids_own]))[None]
    ids_other = swap_core(ids).astype(f32)
    ids = ids.astype(f32)
    own_other, received_other = swap_core(own), swap_core(received)
    grad_own = take(out_grad, near)
    grad_received = swap_ctx(take(out_grad, 1 - near))

    piece = pack_rest(
        proj_weight, up_weight, down_weight,
        (proj_bias, first_gain, first_shift, down_bias, second_gain, second_shift), up_bias, rank,
    )
    piece = lax.dynamic_slice_in_dim(piece, 32 * near, 32, axis=0)
    piece, joint_packed = lax.optimization_barrier((piece, joint_packed))
    sent = jnp.broadcast_to(piece[None], (2 * groups, 32, D))
    packed_a = lax.all_to_all(sent, ("g", "zl"), 0, 0, tiled=True).reshape(groups * 64, D)
    packed_b = swap_core(packed_a)

    choice = joint_choice()
    weight, weight_t, bias, bias_t = call(
        unpack_joint, 2, [((D, 768), bf16), ((768, D), bf16), ((8, 256), f32), ((256, 128), f32)], name="unpack"
    )(joint_packed, jnp.asarray(choice, bf16))

    attention = call(
        attend,
        7,
        [
            ((SEQ, 256), bf16), ((SEQ, 256), bf16), ((SEQ, 256), bf16), ((PART, SEQ), bf16), ((PART, SEQ), bf16),
            ((PART, SEQ), bf16), ((8, SEQ), f32),
        ],
        scratch=[pltpu.VMEM((PART + 16, SEQ), bf16), pltpu.VMEM((SEQ, 128), f32)],
        scalars=1,
        flops=8 * 10**9,
        name="attend",
    )
    kept_other = attention(place, own_other, received_other, weight, weight_t, bias, bias_t, ids_other)
    kept = attention(place, own, received, weight, weight_t, bias, bias_t, ids)
    mixed_b = swap_core(kept_other[5])
    mixed_a = kept[5]

    rest = rest_choice()
    out_own, out_received, attn_own, attn_received, back_a, back_b, packed_keep, packed_send = call(
        feed_forward,
        10,
        [((HALF, D), bf16)] * 4 + [((PART, SEQ), bf16)] * 2 + [((2048, D), bf16)] * 2,
        scratch=[
            pltpu.VMEM((D, D), bf16), pltpu.VMEM((D, FF), bf16), pltpu.VMEM((FF, D), bf16), pltpu.VMEM((D, FF), f32),
            pltpu.VMEM((D, FF), f32), pltpu.VMEM((D, D), f32), pltpu.VMEM((HALF, FF), bf16), pltpu.VMEM((HALF, FF), f32),
        ],
        scalars=1,
        flops=10 * 10**9,
        name="feed_forward",
    )(
        place, own, received, grad_own, grad_received, mixed_a, mixed_b, packed_a, packed_b,
        jnp.asarray(rest, bf16), jnp.asarray(rest.transpose(0, 2, 1), bf16),
    )
    back_other = swap_core(back_b)
    out_back = swap_ctx(out_received)

    packed_got = swap_core(packed_send)

    back_scratch = [
        pltpu.VMEM((PART, SEQ), f32), pltpu.VMEM((SEQ, 256), bf16), pltpu.VMEM((SEQ, 256), bf16),
        pltpu.VMEM((SEQ, 256), bf16), pltpu.VMEM((96, SEQ), bf16), pltpu.VMEM((96, SEQ), bf16),
        pltpu.VMEM((SEQ, 128), f32), pltpu.VMEM((SEQ, D), bf16),
    ]
    partial, totals, bias_totals = call(
        functools.partial(attend_back, False),
        12,
        [((SEQ, D), bf16), ((D, 768), f32), ((8, 256), f32)],
        scratch=back_scratch,
        scalars=1,
        flops=20 * 10**9,
        name="attend_back_own",
    )(place, own, received, weight_t, ids, *kept, back_a)
    rest_sum = (packed_keep.astype(f32) + packed_got.astype(f32)).astype(bf16).reshape(2 * groups, 32, D)
    rest_sum, back_other = lax.optimization_barrier((rest_sum, back_other))
    rest_all = lax.all_to_all(rest_sum, ("g", "zl"), 0, 0, tiled=True)
    partial_other, joint_grads = call(
        functools.partial(attend_back, True),
        15,
        [((SEQ, D), bf16), ((2048, 128), bf16)],
        scratch=back_scratch,
        scalars=1,
        flops=20 * 10**9,
        name="attend_back_other",
    )(place, own_other, received_other, weight_t, ids_other, *kept_other, back_other, totals, bias_totals, jnp.asarray(choice.T, bf16))

    partial_got = swap_core(partial_other)
    whole = partial.astype(f32) + partial_got.astype(f32)
    mine = lax.dynamic_slice_in_dim(whole, HALF * near, HALF, axis=0) + attn_own.astype(f32)
    theirs = lax.dynamic_slice_in_dim(whole, HALF * (1 - near), HALF, axis=0) + attn_received.astype(f32)
    tokens_back = swap_ctx(theirs.astype(bf16))
    mine = mine.astype(bf16)

    def ordered(kept_part, got_part):
        return jnp.where(near == 0, jnp.stack([kept_part, got_part]), jnp.stack([got_part, kept_part]))

    joint_sent = jnp.broadcast_to(
        joint_grads.reshape(groups, 2, 1, 32, 128), (groups, 2, 2, 32, 128)
    ).reshape(4 * groups, 32, 128)
    joint_all = lax.all_to_all(joint_sent, ALL, 0, 0, tiled=True).reshape(groups, 2, 2, 32, 128)
    joint_sum = jnp.sum(joint_all.astype(f32), axis=(0, 2))

    rest_half = jnp.sum(rest_all.reshape(2 * groups, 32, D).astype(f32), axis=0).astype(bf16)
    rest_got = swap_ctx(rest_half)
    rest_whole = jnp.where(
        near == 0, jnp.concatenate([rest_half, rest_got]), jnp.concatenate([rest_got, rest_half])
    ).astype(f32)

    def shard(vector):
        size = vector.shape[0] // RANKS
        return lax.dynamic_slice_in_dim(vector, size * rank, size, axis=0)

    heads, tails = [], []
    for at, (first, tail_row, tail_lane) in enumerate(((0, 18, 0), (6, 18, 64), (12, 24, 0))):
        for side in range(2):
            heads.append(joint_sum[side, first : first + 6, :])
            heads.append(joint_sum[side, tail_row : tail_row + 6, tail_lane : tail_lane + 64])
    qkv_grad = jnp.concatenate(heads, axis=1)
    q_bias_grad, v_bias_grad = (
        shard(jnp.concatenate([joint_sum[0, row], joint_sum[0, end, 64:], joint_sum[1, row], joint_sum[1, end, 64:]]))
        for row, end in ((30, 24), (31, 25))
    )
    proj_grad = rest_whole[0:6]
    up_grad = jnp.concatenate([rest_whole[6 + 6 * block : 12 + 6 * block] for block in range(4)], axis=1)
    down_grad = rest_whole[30:54]
    vectors = [shard(rest_whole[54 + at]) for at in range(6)]
    up_bias_grad = shard(rest_whole[60:64].reshape(FF))
    return (
        ordered(out_own, out_back),
        ordered(mine, tokens_back),
        qkv_grad,
        q_bias_grad,
        v_bias_grad,
        proj_grad,
        vectors[0],
        vectors[1],
        vectors[2],
        up_grad,
        up_bias_grad,
        down_grad,
        vectors[3],
        vectors[4],
        vectors[5],
    )


def solution(mesh):
    grid = Mesh(mesh.devices.reshape(RANKS // 2, 2, 2), ALL)
    ranks = ("g", "c")
    data, matrix, vector = P(ranks, "zl", None), P(ranks, None), P(ranks)
    in_specs = (
        data, P(ranks, "zl"), data, matrix, vector, vector, matrix, vector, vector, vector, matrix, vector, matrix,
        vector, vector, vector,
    )
    out_specs = (
        data, data, matrix, vector, vector, matrix, vector, vector, vector, matrix, vector, matrix, vector, vector,
        vector,
    )
    return jax.shard_map(local, mesh=grid, in_specs=in_specs, out_specs=out_specs, check_vma=False)
```

```python
import functools
import math

import jax
import jax.numpy as jnp
import numpy as np
from jax import lax
from jax.experimental import pallas as pl
from jax.experimental.pallas import tpu as pltpu
from jax.sharding import Mesh
from jax.sharding import PartitionSpec as P

D = 384
FF = 1536
SEQ = 1024
HALF = 512
PART = 192
RANKS = 64
ROWS = D // RANKS
SCALE = 1.0 / math.sqrt(32)
LOG2E = math.log2(math.e)
BOUND = 60.0

bf16 = jnp.bfloat16
f32 = jnp.float32
VMEM = pl.BlockSpec(memory_space=pltpu.VMEM)
SMEM = pl.BlockSpec(memory_space=pltpu.SMEM)
SWAP = ((0, 1), (1, 0))
ALL = ("g", "c", "zl")


def dot(left, right):
    return lax.dot_general(left, right, (((1,), (0,)), ((), ())), preferred_element_type=f32)


def dot_nt(left, right):
    return lax.dot_general(left, right, (((1,), (1,)), ((), ())), preferred_element_type=f32)


def dot_tn(left, right):
    return lax.dot_general(left, right, (((0,), (0,)), ((), ())), preferred_element_type=f32)


def joint_choice():
    choice = np.zeros((256, 256), np.float32)
    for rank in range(8):
        for block in range(5):
            for row in range(ROWS):
                choice[48 * block + ROWS * rank + row, 32 * rank + ROWS * block + row] = 1
        for place, row in ((240, 30), (241, 31), (242, 24), (243, 25)):
            choice[place, 32 * rank + row] = 1
    return choice


def rest_choice():
    choice = np.zeros((2, 448, 256), np.float32)
    for core in range(2):
        for at in range(4):
            rank = 2 * at + core
            for row in range(ROWS):
                for block in range(5):
                    choice[core, 48 * block + ROWS * rank + row, 64 * at + ROWS * block + row] = 1
            for row in range(24):
                choice[core, 240 + 24 * rank + row, 64 * at + 30 + row] = 1
            for row in range(10):
                choice[core, 432 + row, 64 * at + 54 + row] = 1
    return choice


def call(kernel, ins, outs, scratch=(), scalars=0, flops=0, name=None):
    return pl.pallas_call(
        kernel,
        in_specs=[SMEM] * scalars + [VMEM] * ins,
        out_specs=[VMEM] * len(outs),
        out_shape=[jax.ShapeDtypeStruct(shape, dtype) for shape, dtype in outs],
        scratch_shapes=scratch,
        compiler_params=pltpu.CompilerParams(vmem_limit_bytes=56 * 2**20),
        cost_estimate=pl.CostEstimate(flops=flops, bytes_accessed=4 * 2**20, transcendentals=0),
        name=name,
    )


def unpack_joint(packed, choice, weight, weight_t, bias, bias_t):
    low_lanes = lax.broadcasted_iota(jnp.int32, (48, 128), 1) < 64
    total = jnp.zeros((16, 128), f32)
    for step in range(8):
        out = dot(choice[...], packed[256 * step : 256 * step + 256, :])
        rows = slice(48 * step, 48 * step + 48)
        mixed = out[144:192]
        weight[rows, 0:128] = out[0:48].astype(bf16)
        weight[rows, 256:384] = out[48:96].astype(bf16)
        weight[rows, 512:640] = out[96:144].astype(bf16)
        weight[rows, 128:256] = jnp.where(low_lanes, mixed, 0.0).astype(bf16)
        weight[rows, 384:512] = jnp.where(low_lanes, pltpu.roll(mixed, 64, 1), 0.0).astype(bf16)
        weight[rows, 640:768] = jnp.where(low_lanes, out[192:240], 0.0).astype(bf16)
        total = total + out[240:256]
    tail = jnp.where(low_lanes[:16], pltpu.roll(total, 64, 1), 0.0)
    both = jnp.concatenate([total[0:2], jnp.zeros((6, 128), f32)], axis=0)
    tails = jnp.concatenate([tail[2:4], jnp.zeros((6, 128), f32)], axis=0)
    rows = jnp.concatenate([both, tails], axis=1)
    bias[...] = rows
    bias_t[...] = jnp.transpose(jnp.concatenate([rows, jnp.zeros((120, 256), f32)], axis=0))
    weight_t[...] = jnp.transpose(weight[...].astype(f32)).astype(bf16)


def padded_head(matrix, head, lanes, extra=None):
    parts = []
    if head:
        parts.append(jnp.zeros((32 * head, lanes), bf16))
    parts.append(matrix)
    if extra is None:
        parts.append(jnp.zeros((224 - 32 * head, lanes), bf16))
    else:
        if head < 5:
            parts.append(jnp.zeros((160 - 32 * head, lanes), bf16))
        parts.append(extra)
        parts.append(jnp.zeros((48, lanes), bf16))
    return jnp.concatenate(parts, axis=0)


def id_columns(id_row):
    return jnp.transpose(jnp.broadcast_to(id_row, (128, SEQ)))


def attend(place, own, received, weight, weight_t, bias, bias_t, id_row, q_rows, k_rows, v_rows, q_t, k_t, mixed_t, lse, v_t, ids_t):
    lane = lax.broadcasted_iota(jnp.int32, (HALF, 256), 1) < PART
    for half, block in ((place[0], own), (1 - place[0], received)):
        at = pl.ds(pl.multiple_of(half * HALF, HALF), HALF)
        tokens = block[...]
        flat = dot(tokens, weight[...])
        q_rows[at, :] = ((flat[:, 0:256] + bias[0:1, :]) * (SCALE * LOG2E)).astype(bf16)
        k_rows[at, :] = jnp.where(lane, flat[:, 256:512], 1.0).astype(bf16)
        v_rows[at, :] = jnp.where(lane, flat[:, 512:768] + bias[1:2, :], 1.0).astype(bf16)
        q_t[:, at] = ((dot_nt(weight_t[0:PART, :], tokens) + bias_t[0:PART, 0:1]) * (SCALE * LOG2E)).astype(bf16)
        k_t[:, at] = dot_nt(weight_t[256 : 256 + PART, :], tokens).astype(bf16)
        v_t[0:PART, at] = (dot_nt(weight_t[512 : 512 + PART, :], tokens) + bias_t[0:PART, 1:2]).astype(bf16)
    v_t[PART:, :] = jnp.ones((16, SEQ), bf16)
    ids_t[...] = id_columns(id_row[...])
    lse[...] = jnp.zeros_like(lse)
    largest = jnp.zeros((), f32)
    for head in range(6):
        rows = slice(32 * head, 32 * head + 32)
        q_size = jnp.max(jnp.sum(jnp.square(q_t[rows, :].astype(f32)), axis=0, keepdims=True))
        k_size = jnp.max(jnp.sum(jnp.square(k_t[rows, :].astype(f32)), axis=0, keepdims=True))
        largest = jnp.maximum(largest, q_size * k_size)

    def run(shift):
        def step(tile, carried):
            at = pl.ds(pl.multiple_of(tile * HALF, HALF), HALF)
            same = jnp.concatenate([ids_t[...]] * 4, axis=1) == id_row[:, at]
            keep = same.astype(f32).astype(bf16)
            for head in range(6):
                rows = slice(32 * head, 32 * head + 32)
                scores = dot(k_rows[...], padded_head(q_t[rows, at], head, HALF))
                if shift:
                    scores = jnp.where(same, scores, -1e30)
                    top = jnp.max(scores, axis=0, keepdims=True)
                    probs = jnp.exp2(scores - top).astype(bf16)
                else:
                    top = 0.0
                    probs = jnp.exp2(scores).astype(bf16) * keep
                mixed = dot(jnp.concatenate([v_t[rows, :], v_t[PART:, :]], axis=0), probs)
                total = mixed[32:33]
                mixed_t[rows, at] = (mixed[0:32] * (1.0 / total)).astype(bf16)
                lse[head : head + 1, at] = jnp.log2(total) + top
            return carried

        lax.fori_loop(0, SEQ // HALF, step, 0)

    @pl.when(largest <= BOUND * BOUND)
    def _():
        run(False)

    @pl.when(jnp.logical_not(largest <= BOUND * BOUND))
    def _():
        run(True)


def three_terms(row):
    first = row.astype(bf16).astype(f32)
    second = (row - first).astype(bf16).astype(f32)
    third = row - first - second
    return jnp.concatenate([first, second, third, jnp.zeros((13, row.shape[1]), f32)], axis=0).astype(bf16)


def attend_back(
    has_totals, place, own, received, weight_t, id_row, q_rows, k_rows, v_rows, q_t, k_t, mixed_t, lse, mixed_grad_t, *rest
):
    if has_totals:
        totals_in, bias_in, choice, tokens_grad, packed, q_grad_t, k_grad, v_grad, grad_rows, q_extra, o_extra, ids_t, x_rows = rest
    else:
        tokens_grad, totals_out, bias_out, q_grad_t, k_grad, v_grad, grad_rows, q_extra, o_extra, ids_t, x_rows = rest
    for half, block in ((place[0], own), (1 - place[0], received)):
        x_rows[pl.ds(pl.multiple_of(half * HALF, HALF), HALF), :] = block[...]
    ids_t[...] = id_columns(id_row[...])
    grad_rows[:, 0:PART] = jnp.transpose(mixed_grad_t[...].astype(f32)).astype(bf16)
    grad_rows[:, PART:] = jnp.zeros((SEQ, 256 - PART), bf16)
    for head in range(6):
        rows = slice(32 * head, 32 * head + 32)
        delta = jnp.sum(mixed_grad_t[rows, :].astype(f32) * mixed_t[rows, :].astype(f32), axis=0, keepdims=True)
        q_extra[16 * head : 16 * head + 16, :] = three_terms(-lse[head : head + 1, :])
        o_extra[16 * head : 16 * head + 16, :] = three_terms(-delta)
    q_grad_t[...] = jnp.zeros_like(q_grad_t)
    lane = lax.broadcasted_iota(jnp.int32, (SEQ, 256), 1)

    def step(tile, carried):
        at = pl.ds(pl.multiple_of(tile * 256, 256), 256)
        ids = ids_t[at, :]
        keep = (jnp.concatenate([ids] * 8, axis=1) == id_row[...]).astype(f32).astype(bf16)
        key_total = jnp.zeros((256, 256), f32)
        value_total = jnp.zeros((256, 256), f32)
        for head in range(6):
            rows = slice(32 * head, 32 * head + 32)
            extra = slice(16 * head, 16 * head + 16)
            inside = (lane >= 32 * head) & (lane < 32 * head + 32)
            scores = dot(k_rows[at, :], padded_head(q_t[rows, :], head, SEQ, q_extra[extra, :]))
            probs = jnp.exp2(jnp.minimum(scores, 1.0)).astype(bf16) * keep
            spread = dot(v_rows[at, :], padded_head(mixed_grad_t[rows, :], head, SEQ, o_extra[extra, :]))
            scores_grad = probs * spread.astype(bf16)
            key_total += dot(scores_grad, jnp.where(inside, q_rows[...], jnp.zeros_like(q_rows[...])))
            value_total += dot(probs, jnp.where(inside, grad_rows[...], jnp.zeros_like(grad_rows[...])))
            q_grad_t[rows, :] += dot(k_t[rows, at], scores_grad)
        k_grad[at, :] = (key_total * (1.0 / LOG2E)).astype(bf16)
        v_grad[at, :] = value_total.astype(bf16)
        return carried

    lax.fori_loop(0, SEQ // 256, step, 0)
    grad_rows[:, 0:PART] = jnp.transpose(q_grad_t[...] * SCALE).astype(bf16)
    tokens_grad[...] = (
        dot(grad_rows[:, 0:PART], weight_t[0:PART, :])
        + dot(k_grad[:, 0:PART], weight_t[256 : 256 + PART, :])
        + dot(v_grad[:, 0:PART], weight_t[512 : 512 + PART, :])
    ).astype(bf16)
    totals = [dot_tn(x_rows[...], part[...]) for part in (grad_rows, k_grad, v_grad)]
    bias_rows = jnp.concatenate(
        [jnp.sum(part[...].astype(f32), axis=0, keepdims=True) for part in (grad_rows, v_grad)]
        + [jnp.zeros((6, 256), f32)],
        axis=0,
    )
    if not has_totals:
        for at, part in enumerate(totals):
            totals_out[:, 256 * at : 256 * at + 256] = part
        bias_out[...] = bias_rows
        return
    q_all, k_all, v_all = (part + totals_in[:, 256 * at : 256 * at + 256] for at, part in enumerate(totals))
    bias_rows = bias_rows + bias_in[...]
    low_lanes = lax.broadcasted_iota(jnp.int32, (D, 128), 1) < 64
    fourth = jnp.where(low_lanes, q_all[:, 128:], pltpu.roll(k_all[:, 128:], 64, 1))
    fifth = jnp.where(low_lanes, v_all[:, 128:], 0.0)
    ends = jnp.where(low_lanes[:8], 0.0, pltpu.roll(bias_rows[:, 128:], 64, 1))
    biases = jnp.concatenate([bias_rows[0:2, 0:128], ends[0:2], jnp.zeros((12, 128), f32)], axis=0)
    for step_at in range(8):
        rows = slice(48 * step_at, 48 * step_at + 48)
        stacked = jnp.concatenate(
            [q_all[rows, 0:128], k_all[rows, 0:128], v_all[rows, 0:128], fourth[rows], fifth[rows], biases], axis=0
        ).astype(bf16)
        packed[256 * step_at : 256 * step_at + 256, :] = dot(choice[...], stacked).astype(bf16)


def normal_parts(values):
    mean = jnp.mean(values, axis=-1, keepdims=True)
    centered = values - mean
    scale = lax.rsqrt(jnp.mean(centered * centered, axis=-1, keepdims=True) + 1e-05)
    return centered * scale, scale


def normal_back(cotangent, normal, scale, gain):
    weighted = cotangent * gain
    mean = jnp.mean(weighted, axis=-1, keepdims=True)
    along = jnp.mean(weighted * normal, axis=-1, keepdims=True)
    return scale * (weighted - mean - normal * along)


def column_sum(matrix):
    return jnp.sum(matrix.astype(f32), axis=0, keepdims=True)


def feed_forward(
    place, own, received, own_grad, received_grad, mixed_a, mixed_b, packed_a, packed_b, choice, choice_t,
    out_own, out_received, attn_own, attn_received, back_a, back_b, packed_keep, packed_send,
    proj, up, down, up_total, down_total_t, proj_total, activated, slope,
):
    core, near = place[1], place[0]
    vectors = jnp.zeros((16, D), f32)
    for step in range(8):
        rows = slice(256 * step, 256 * step + 256)
        out = dot(choice[core], packed_a[rows, :]) + dot(choice[1 - core], packed_b[rows, :])
        proj[48 * step : 48 * step + 48, :] = out[0:48].astype(bf16)
        for block in range(4):
            up[48 * step : 48 * step + 48, D * block : D * block + D] = out[48 + 48 * block : 96 + 48 * block].astype(bf16)
        down[192 * step : 192 * step + 192, :] = out[240:432].astype(bf16)
        vectors = vectors + out[432:448]
    proj_bias, first_gain, first_shift, down_bias, second_gain, second_shift = (vectors[i : i + 1] for i in range(6))
    up_bias = jnp.concatenate([vectors[i : i + 1] for i in range(6, 10)], axis=1)
    rows_a = pl.ds(pl.multiple_of(core * PART, PART), PART)
    rows_b = pl.ds(pl.multiple_of((1 - core) * PART, PART), PART)
    sums = None
    for number, (half, block, grad_block, out_block, attn_block) in enumerate(
        ((near, own, own_grad, out_own, attn_own), (1 - near, received, received_grad, out_received, attn_received))
    ):
        at = pl.ds(pl.multiple_of(half * HALF, HALF), HALF)
        heads_a, heads_b = mixed_a[:, at], mixed_b[:, at]
        residual = block[...].astype(f32) + (dot_tn(heads_a, proj[rows_a, :]) + dot_tn(heads_b, proj[rows_b, :]) + proj_bias)
        first_normal, first_scale = normal_parts(residual)
        first_norm = first_normal * first_gain + first_shift
        first_low = first_norm.astype(bf16)
        for col in range(4):
            cols = slice(D * col, D * col + D)
            hidden = dot(first_low, up[:, cols]) + up_bias[:, cols]
            bell = jnp.exp2(hidden * hidden * (-0.5 * LOG2E))
            inner = 1.0 / (1.0 + jnp.abs(hidden) * (0.3275911 / math.sqrt(2)))
            series = inner * (0.127414796 + inner * (-0.142248368 + inner * (0.7107068705 + inner * (-0.7265760135 + inner * 0.5307027145))))
            tail = series * bell
            below = jnp.where(hidden >= 0.0, 1.0 - tail, tail)
            activated[:, cols] = (hidden * below).astype(bf16)
            slope[:, cols] = below + hidden * bell * (1.0 / math.sqrt(2 * math.pi))
        second_sum = first_norm + (dot(activated[...], down[...]) + down_bias)
        second_normal, second_scale = normal_parts(second_sum)
        out_block[...] = (second_normal * second_gain + second_shift).astype(bf16)
        out_grad = grad_block[...].astype(f32)
        second_grad = normal_back(out_grad, second_normal, second_scale, second_gain)
        branch_grad = second_grad.astype(bf16)
        first_grad = second_grad
        up_bias_grads = []
        for col in range(4):
            cols = slice(D * col, D * col + D)
            up_grad = (dot_nt(branch_grad, down[cols, :]) * slope[:, cols]).astype(bf16)
            first_grad = first_grad + dot_nt(up_grad, up[:, cols])
            up_bias_grads.append(column_sum(up_grad))
            up_new = dot_tn(first_low, up_grad)
            down_new = dot_tn(branch_grad, activated[:, cols])
            if number == 0:
                up_total[:, cols] = up_new
                down_total_t[:, cols] = down_new
            else:
                up_total[:, cols] += up_new
                down_total_t[:, cols] += down_new
        residual_grad = normal_back(first_grad, first_normal, first_scale, first_gain)
        attn_grad = residual_grad.astype(bf16)
        attn_block[...] = attn_grad
        back_a[:, at] = dot_nt(proj[rows_a, :], attn_grad).astype(bf16)
        back_b[:, at] = dot_nt(proj[rows_b, :], attn_grad).astype(bf16)
        new_a, new_b = dot(heads_a, attn_grad), dot(heads_b, attn_grad)
        if number == 0:
            proj_total[rows_a, :] = new_a
            proj_total[rows_b, :] = new_b
        else:
            proj_total[rows_a, :] += new_a
            proj_total[rows_b, :] += new_b
        new = [
            column_sum(attn_grad),
            column_sum(first_grad * first_normal),
            column_sum(first_grad),
            column_sum(branch_grad),
            column_sum(out_grad * second_normal),
            column_sum(out_grad),
        ] + up_bias_grads
        sums = new if sums is None else [a + b for a, b in zip(sums, new)]
    vector_rows = jnp.concatenate(sums + [jnp.zeros((6, D), f32)], axis=0)
    for pair in range(4):
        down_rows = jnp.transpose(down_total_t[:, D * pair : D * pair + D])
        for inner_step in range(2):
            step = 2 * pair + inner_step
            rows = slice(48 * step, 48 * step + 48)
            stacked = jnp.concatenate(
                [proj_total[rows, :]]
                + [up_total[rows, D * block : D * block + D] for block in range(4)]
                + [down_rows[192 * inner_step : 192 * inner_step + 192], vector_rows],
                axis=0,
            ).astype(bf16)
            packed_rows = slice(256 * step, 256 * step + 256)
            packed_keep[packed_rows, :] = dot(choice_t[core], stacked).astype(bf16)
            packed_send[packed_rows, :] = dot(choice_t[1 - core], stacked).astype(bf16)


def swap_core(value):
    return lax.ppermute(value, "c", SWAP)


def swap_ctx(value):
    return lax.ppermute(value, "zl", SWAP)


def spread_out(vector, rank):
    size = vector.shape[0]
    return lax.dynamic_update_slice(jnp.zeros((size * RANKS,), bf16), vector, (size * rank,))


def pack_joint(qkv_weight, query_bias, value_bias, rank):
    query_all, value_all = spread_out(query_bias, rank), spread_out(value_bias, rank)
    pieces = []
    for core in range(2):
        q, k, v = (qkv_weight[:, D * at + PART * core : D * at + PART * core + PART] for at in range(3))
        q_bias, v_bias = (part[PART * core : PART * core + PART] for part in (query_all, value_all))
        ends = jnp.concatenate([q_bias[None, 128:], v_bias[None, 128:], jnp.zeros((4, 64), bf16)], axis=0)
        pieces.append(
            jnp.concatenate(
                [
                    q[:, :128],
                    k[:, :128],
                    v[:, :128],
                    jnp.concatenate([q[:, 128:], k[:, 128:]], axis=1),
                    jnp.concatenate([v[:, 128:], ends], axis=1),
                    q_bias[None, :128],
                    v_bias[None, :128],
                ],
                axis=0,
            )
        )
    return jnp.stack(pieces)


def pack_rest(proj_weight, up_weight, down_weight, vectors, up_bias, rank):
    return jnp.concatenate(
        [proj_weight]
        + [up_weight[:, D * block : D * block + D] for block in range(4)]
        + [down_weight]
        + [spread_out(vector, rank)[None] for vector in vectors]
        + [spread_out(up_bias, rank).reshape(4, D)],
        axis=0,
    )


def local(
    tokens, segment_ids, out_grad, qkv_weight, query_bias, value_bias, proj_weight, proj_bias, first_gain, first_shift,
    up_weight, up_bias, down_weight, down_bias, second_gain, second_shift,
):
    group, core, near = (lax.axis_index(name) for name in ALL)
    rank = 2 * group + core
    groups = RANKS // 2
    place = jnp.stack([near, core]).astype(jnp.int32)
    take = functools.partial(lax.dynamic_index_in_dim, axis=0, keepdims=False)

    piece = pack_joint(qkv_weight, query_bias, value_bias, rank)
    piece = lax.dynamic_slice_in_dim(piece, 16 * near, 16, axis=1)
    sent = jnp.broadcast_to(piece[None, :, None], (groups, 2, 2, 16, 128)).reshape(4 * groups, 16, 128)
    joint_packed = lax.all_to_all(sent, ALL, 0, 0, tiled=True).reshape(groups * 64, 128)

    own = take(tokens, near)
    received = swap_ctx(take(tokens, 1 - near))
    ids_own = take(segment_ids, near)
    ids_received = swap_ctx(take(segment_ids, 1 - near))
    ids = jnp.where(near == 0, jnp.concatenate([ids_own, ids_received]), jnp.concatenate([ids_received, ids_own]))[None]
    ids_other = swap_core(ids).astype(f32)
    ids = ids.astype(f32)
    own_other, received_other = swap_core(own), swap_core(received)
    grad_own = take(out_grad, near)
    grad_sent = take(out_grad, 1 - near)

    piece = pack_rest(
        proj_weight, up_weight, down_weight,
        (proj_bias, first_gain, first_shift, down_bias, second_gain, second_shift), up_bias, rank,
    )
    piece = lax.dynamic_slice_in_dim(piece, 32 * near, 32, axis=0)
    sent = jnp.broadcast_to(piece[None], (2 * groups, 32, D))
    sent, grad_sent, joint_packed, received, received_other, own_other, ids_other = lax.optimization_barrier(
        (sent, grad_sent, joint_packed, received, received_other, own_other, ids_other)
    )
    grad_received = swap_ctx(grad_sent)
    packed_a = lax.all_to_all(sent, ("g", "zl"), 0, 0, tiled=True).reshape(groups * 64, D)
    choice = joint_choice()
    weight, weight_t, bias, bias_t = call(
        unpack_joint, 2, [((D, 768), bf16), ((768, D), bf16), ((8, 256), f32), ((256, 128), f32)], name="unpack"
    )(joint_packed, jnp.asarray(choice, bf16))

    attention = call(
        attend,
        7,
        [
            ((SEQ, 256), bf16), ((SEQ, 256), bf16), ((SEQ, 256), bf16), ((PART, SEQ), bf16), ((PART, SEQ), bf16),
            ((PART, SEQ), bf16), ((8, SEQ), f32),
        ],
        scratch=[pltpu.VMEM((PART + 16, SEQ), bf16), pltpu.VMEM((SEQ, 128), f32)],
        scalars=1,
        flops=8 * 10**9,
        name="attend",
    )
    kept_other = attention(place, own_other, received_other, weight, weight_t, bias, bias_t, ids_other)
    *kept_other, packed_a, own = lax.optimization_barrier((*kept_other, packed_a, own))
    packed_b = swap_core(packed_a)
    kept = attention(place, own, received, weight, weight_t, bias, bias_t, ids)
    mixed_b = swap_core(kept_other[5])
    mixed_a = kept[5]

    rest = rest_choice()
    out_own, out_received, attn_own, attn_received, back_a, back_b, packed_keep, packed_send = call(
        feed_forward,
        10,
        [((HALF, D), bf16)] * 4 + [((PART, SEQ), bf16)] * 2 + [((2048, D), bf16)] * 2,
        scratch=[
            pltpu.VMEM((D, D), bf16), pltpu.VMEM((D, FF), bf16), pltpu.VMEM((FF, D), bf16), pltpu.VMEM((D, FF), f32),
            pltpu.VMEM((D, FF), f32), pltpu.VMEM((D, D), f32), pltpu.VMEM((HALF, FF), bf16), pltpu.VMEM((HALF, FF), f32),
        ],
        scalars=1,
        flops=10 * 10**9,
        name="feed_forward",
    )(
        place, own, received, grad_own, grad_received, mixed_a, mixed_b, packed_a, packed_b,
        jnp.asarray(rest, bf16), jnp.asarray(rest.transpose(0, 2, 1), bf16),
    )
    back_other = swap_core(back_b)
    out_back = swap_ctx(out_received)

    packed_got = swap_core(packed_send)

    back_scratch = [
        pltpu.VMEM((PART, SEQ), f32), pltpu.VMEM((SEQ, 256), bf16), pltpu.VMEM((SEQ, 256), bf16),
        pltpu.VMEM((SEQ, 256), bf16), pltpu.VMEM((96, SEQ), bf16), pltpu.VMEM((96, SEQ), bf16),
        pltpu.VMEM((SEQ, 128), f32), pltpu.VMEM((SEQ, D), bf16),
    ]
    partial, totals, bias_totals = call(
        functools.partial(attend_back, False),
        12,
        [((SEQ, D), bf16), ((D, 768), f32), ((8, 256), f32)],
        scratch=back_scratch,
        scalars=1,
        flops=20 * 10**9,
        name="attend_back_own",
    )(place, own, received, weight_t, ids, *kept, back_a)
    partial, totals, bias_totals, packed_got, back_other, out_back = lax.optimization_barrier(
        (partial, totals, bias_totals, packed_got, back_other, out_back)
    )
    rest_sum = (packed_keep.astype(f32) + packed_got.astype(f32)).astype(bf16).reshape(2 * groups, 32, D)
    rest_all = lax.all_to_all(rest_sum, ("g", "zl"), 0, 0, tiled=True)
    partial_other, joint_grads = call(
        functools.partial(attend_back, True),
        15,
        [((SEQ, D), bf16), ((2048, 128), bf16)],
        scratch=back_scratch,
        scalars=1,
        flops=20 * 10**9,
        name="attend_back_other",
    )(place, own_other, received_other, weight_t, ids_other, *kept_other, back_other, totals, bias_totals, jnp.asarray(choice.T, bf16))

    joint_grads, partial_other, rest_all = lax.optimization_barrier((joint_grads, partial_other, rest_all))

    partial_got = swap_core(partial_other)
    whole = partial.astype(f32) + partial_got.astype(f32)
    mine = lax.dynamic_slice_in_dim(whole, HALF * near, HALF, axis=0) + attn_own.astype(f32)
    theirs = lax.dynamic_slice_in_dim(whole, HALF * (1 - near), HALF, axis=0) + attn_received.astype(f32)
    tokens_back = swap_ctx(theirs.astype(bf16))
    mine = mine.astype(bf16)

    def ordered(kept_part, got_part):
        return jnp.where(near == 0, jnp.stack([kept_part, got_part]), jnp.stack([got_part, kept_part]))

    joint_sent = jnp.broadcast_to(
        joint_grads.reshape(groups, 2, 1, 32, 128), (groups, 2, 2, 32, 128)
    ).reshape(4 * groups, 32, 128)
    joint_all = lax.all_to_all(joint_sent, ALL, 0, 0, tiled=True).reshape(groups, 2, 2, 32, 128)
    joint_sum = jnp.sum(joint_all.astype(f32), axis=(0, 2))

    rest_half = jnp.sum(rest_all.reshape(2 * groups, 32, D).astype(f32), axis=0).astype(bf16)
    rest_got = swap_ctx(rest_half)
    rest_whole = jnp.where(
        near == 0, jnp.concatenate([rest_half, rest_got]), jnp.concatenate([rest_got, rest_half])
    ).astype(f32)

    def shard(vector):
        size = vector.shape[0] // RANKS
        return lax.dynamic_slice_in_dim(vector, size * rank, size, axis=0)

    heads, tails = [], []
    for at, (first, tail_row, tail_lane) in enumerate(((0, 18, 0), (6, 18, 64), (12, 24, 0))):
        for side in range(2):
            heads.append(joint_sum[side, first : first + 6, :])
            heads.append(joint_sum[side, tail_row : tail_row + 6, tail_lane : tail_lane + 64])
    qkv_grad = jnp.concatenate(heads, axis=1)
    q_bias_grad, v_bias_grad = (
        shard(jnp.concatenate([joint_sum[0, row], joint_sum[0, end, 64:], joint_sum[1, row], joint_sum[1, end, 64:]]))
        for row, end in ((30, 24), (31, 25))
    )
    proj_grad = rest_whole[0:6]
    up_grad = jnp.concatenate([rest_whole[6 + 6 * block : 12 + 6 * block] for block in range(4)], axis=1)
    down_grad = rest_whole[30:54]
    vectors = [shard(rest_whole[54 + at]) for at in range(6)]
    up_bias_grad = shard(rest_whole[60:64].reshape(FF))
    return (
        ordered(out_own, out_back),
        ordered(mine, tokens_back),
        qkv_grad,
        q_bias_grad,
        v_bias_grad,
        proj_grad,
        vectors[0],
        vectors[1],
        vectors[2],
        up_grad,
        up_bias_grad,
        down_grad,
        vectors[3],
        vectors[4],
        vectors[5],
    )


def solution(mesh):
    grid = Mesh(mesh.devices.reshape(RANKS // 2, 2, 2), ALL)
    ranks = ("g", "c")
    data, matrix, vector = P(ranks, "zl", None), P(ranks, None), P(ranks)
    in_specs = (
        data, P(ranks, "zl"), data, matrix, vector, vector, matrix, vector, vector, vector, matrix, vector, matrix,
        vector, vector, vector,
    )
    out_specs = (
        data, data, matrix, vector, vector, matrix, vector, vector, vector, matrix, vector, matrix, vector, vector,
        vector,
    )
    return jax.shard_map(local, mesh=grid, in_specs=in_specs, out_specs=out_specs, check_vma=False)
```

```python
import functools
import math

import jax
import jax.numpy as jnp
import numpy as np
from jax import lax
from jax.experimental import pallas as pl
from jax.experimental.pallas import tpu as pltpu
from jax.sharding import Mesh
from jax.sharding import PartitionSpec as P

D = 384
FF = 1536
SEQ = 1024
HALF = 512
PART = 192
RANKS = 64
ROWS = D // RANKS
SCALE = 1.0 / math.sqrt(32)
LOG2E = math.log2(math.e)
BOUND = 60.0
TILE = 256
FFN_ROWS = 512
WIDTHS = (3, 5, 8)

bf16 = jnp.bfloat16
f32 = jnp.float32
VMEM = pl.BlockSpec(memory_space=pltpu.VMEM)
SMEM = pl.BlockSpec(memory_space=pltpu.SMEM)
FAR = pl.BlockSpec(memory_space=pl.ANY)
SWAP = ((0, 1), (1, 0))
ALL = ("x", "y", "zh", "c", "zl")


def dot(left, right):
    return lax.dot_general(left, right, (((1,), (0,)), ((), ())), preferred_element_type=f32)


def dot_nt(left, right):
    return lax.dot_general(left, right, (((1,), (1,)), ((), ())), preferred_element_type=f32)


def dot_tn(left, right):
    return lax.dot_general(left, right, (((0,), (0,)), ((), ())), preferred_element_type=f32)


def joint_choice():
    choice = np.zeros((256, 256), np.float32)
    for rank in range(8):
        for block in range(5):
            for row in range(ROWS):
                choice[48 * block + ROWS * rank + row, 32 * rank + ROWS * block + row] = 1
        for place, row in ((240, 30), (241, 31), (242, 24), (243, 25)):
            choice[place, 32 * rank + row] = 1
    return choice


def rest_choice():
    choice = np.zeros((2, 448, 256), np.float32)
    for core in range(2):
        for at in range(4):
            rank = 2 * at + core
            for row in range(ROWS):
                for block in range(5):
                    choice[core, 48 * block + ROWS * rank + row, 64 * at + ROWS * block + row] = 1
            for row in range(24):
                choice[core, 240 + 24 * rank + row, 64 * at + 30 + row] = 1
            for row in range(10):
                choice[core, 432 + row, 64 * at + 54 + row] = 1
    return choice


def call(kernel, ins, outs, scratch=(), scalars=0, flops=0, name=None, far_ins=0, far_outs=0, limit=56):
    return pl.pallas_call(
        kernel,
        in_specs=[SMEM] * scalars + [VMEM] * (ins - far_ins) + [FAR] * far_ins,
        out_specs=[VMEM] * (len(outs) - far_outs) + [FAR] * far_outs,
        out_shape=[jax.ShapeDtypeStruct(shape, dtype) for shape, dtype in outs],
        scratch_shapes=scratch,
        compiler_params=pltpu.CompilerParams(vmem_limit_bytes=limit * 2**20),
        cost_estimate=pl.CostEstimate(flops=flops, bytes_accessed=4 * 2**20, transcendentals=0),
        name=name,
    )


def unpack_joint(packed, choice, weight, weight_t, bias, bias_t):
    low_lanes = lax.broadcasted_iota(jnp.int32, (48, 128), 1) < 64
    total = jnp.zeros((16, 128), f32)
    for step in range(8):
        out = dot(choice[...], packed[256 * step : 256 * step + 256, :])
        rows = slice(48 * step, 48 * step + 48)
        mixed = out[144:192]
        weight[rows, 0:128] = out[0:48].astype(bf16)
        weight[rows, 256:384] = out[48:96].astype(bf16)
        weight[rows, 512:640] = out[96:144].astype(bf16)
        weight[rows, 128:256] = jnp.where(low_lanes, mixed, 0.0).astype(bf16)
        weight[rows, 384:512] = jnp.where(low_lanes, pltpu.roll(mixed, 64, 1), 0.0).astype(bf16)
        weight[rows, 640:768] = jnp.where(low_lanes, out[192:240], 0.0).astype(bf16)
        total = total + out[240:256]
    tail = jnp.where(low_lanes[:16], pltpu.roll(total, 64, 1), 0.0)
    both = jnp.concatenate([total[0:2], jnp.zeros((6, 128), f32)], axis=0)
    tails = jnp.concatenate([tail[2:4], jnp.zeros((6, 128), f32)], axis=0)
    rows = jnp.concatenate([both, tails], axis=1)
    bias[...] = rows
    bias_t[...] = jnp.transpose(jnp.concatenate([rows, jnp.zeros((120, 256), f32)], axis=0))
    weight_t[...] = jnp.transpose(weight[...].astype(f32)).astype(bf16)


def padded_head(matrix, head, lanes, extra=None):
    parts = []
    if head:
        parts.append(jnp.zeros((32 * head, lanes), bf16))
    parts.append(matrix)
    if extra is None:
        parts.append(jnp.zeros((224 - 32 * head, lanes), bf16))
    else:
        if head < 5:
            parts.append(jnp.zeros((160 - 32 * head, lanes), bf16))
        parts.append(extra)
        parts.append(jnp.zeros((48, lanes), bf16))
    return jnp.concatenate(parts, axis=0)


def id_columns(id_row):
    return jnp.transpose(jnp.broadcast_to(id_row, (128, SEQ)))


def met(spans, one, other):
    def reached(tile, by):
        return (2 * tile + 1 >= spans[0, by]) & (2 * tile < spans[0, by] + spans[1, by])

    return reached(one, other) | reached(other, one)


def attend(
    place, spans, own, received, weight, weight_t, bias, bias_t, id_row,
    q_rows, v_rows, k_t, mixed_t, inverse, probs_far, q_t, k_rows, v_t, ids_t, probs_t, sems,
):
    lane = lax.broadcasted_iota(jnp.int32, (HALF, 256), 1) < PART
    for half, block in ((place[0], own), (1 - place[0], received)):
        at = pl.ds(pl.multiple_of(half * HALF, HALF), HALF)
        tokens = block[...]
        flat = dot(tokens, weight[...])
        q_rows[at, :] = ((flat[:, 0:256] + bias[0:1, :]) * (SCALE * LOG2E)).astype(bf16)
        k_rows[at, :] = flat[:, 256:512].astype(bf16)
        v_rows[at, :] = jnp.where(lane, flat[:, 512:768] + bias[1:2, :], 1.0).astype(bf16)
        q_t[:, at] = ((dot_nt(weight_t[0:PART, :], tokens) + bias_t[0:PART, 0:1]) * (SCALE * LOG2E)).astype(bf16)
        k_t[:, at] = dot_nt(weight_t[256 : 256 + PART, :], tokens).astype(bf16)
        v_t[0:PART, at] = (dot_nt(weight_t[512 : 512 + PART, :], tokens) + bias_t[0:PART, 1:2]).astype(bf16)
    v_t[PART:, :] = jnp.ones((16, SEQ), bf16)
    ids_t[...] = id_columns(id_row[...])
    inverse[...] = jnp.ones_like(inverse)
    largest = jnp.zeros((), f32)
    for head in range(6):
        rows = slice(32 * head, 32 * head + 32)
        q_size = jnp.max(jnp.sum(jnp.square(q_t[rows, :].astype(f32)), axis=0, keepdims=True))
        k_size = jnp.max(jnp.sum(jnp.square(k_t[rows, :].astype(f32)), axis=0, keepdims=True))
        largest = jnp.maximum(largest, q_size * k_size)
    small = largest <= BOUND * BOUND

    def tile_of(tile, width, start, shift):
        at = pl.ds(pl.multiple_of(tile * TILE, TILE), TILE)
        keys = pl.ds(pl.multiple_of(start * 128, 128), 128 * width)
        slot = lax.rem(tile, 2)
        if width < 8:
            for block in range(8):

                @pl.when((block < start) | (block >= start + width))
                def _():
                    probs_t[slot, :, 128 * block : 128 * block + 128, :] = jnp.zeros((6, 128, TILE), bf16)

        same = jnp.concatenate([ids_t[keys, :]] * 2, axis=1) == id_row[:, at]
        keep = same.astype(f32).astype(bf16)

        def score(head):
            return dot(k_rows[keys, :], padded_head(q_t[32 * head : 32 * head + 32, at], head, TILE))

        ahead = [score(0)]
        for head in range(6):
            rows = slice(32 * head, 32 * head + 32)
            if head < 5:
                ahead.append(score(head + 1))
            scores = ahead[head]
            if shift:
                scores = jnp.where(same, scores, -1e30)
                probs = jnp.exp2(scores - jnp.max(scores, axis=0, keepdims=True)).astype(bf16)
            else:
                probs = jnp.exp2(scores).astype(bf16) * keep
            probs_t[slot, head, keys, :] = probs
            mixed = dot(jnp.concatenate([v_t[rows, keys], v_t[PART:, keys]], axis=0), probs)
            over = 1.0 / mixed[32:33]
            mixed_t[rows, at] = (mixed[0:32] * over).astype(bf16)
            inverse[head : head + 1, at] = over

    def copies(tile, go):
        slot = lax.rem(tile, 2)
        for other in range(SEQ // TILE):

            @pl.when(met(spans, tile, other))
            def _():
                copy = pltpu.make_async_copy(
                    probs_t.at[slot, :, TILE * other : TILE * other + TILE, :], probs_far.at[tile, other], sems.at[slot, other]
                )
                copy.start() if go else copy.wait()

    def step(tile, carried):
        @pl.when(tile >= 2)
        def _():
            copies(tile - 2, False)

        for width in WIDTHS:

            @pl.when(small & (spans[1, tile] == width))
            def _():
                tile_of(tile, width, spans[0, tile], False)

        @pl.when(jnp.logical_not(small))
        def _():
            tile_of(tile, 8, 0, True)

        copies(tile, True)
        return carried

    lax.fori_loop(0, SEQ // TILE, step, 0)
    for tile in range(SEQ // TILE - 2, SEQ // TILE):
        copies(tile, False)


def three_terms(row):
    first = row.astype(bf16).astype(f32)
    second = (row - first).astype(bf16).astype(f32)
    third = row - first - second
    return jnp.concatenate([first, second, third, jnp.zeros((13, row.shape[1]), f32)], axis=0).astype(bf16)


def attend_back(
    place, spans_a, spans_b, own, received, weight_t,
    q_rows_a, v_rows_a, k_t_a, mixed_t_a, inverse_a, grad_a, q_rows_b, v_rows_b, k_t_b, mixed_t_b, inverse_b, grad_b,
    own_b, received_b, choice, probs_a, probs_b, tokens_a, tokens_b, packed, q_grad, k_grad, v_grad, x_rows, all_totals, *scratch,
):
    back_of(
        spans_a, weight_t, q_rows_a, v_rows_a, k_t_a, mixed_t_a, inverse_a, grad_a, probs_a, tokens_a, q_grad, k_grad, v_grad,
        *scratch,
    )
    totals, first_bias = joint_totals(place, own, received, x_rows, q_grad, k_grad, v_grad)
    for at, part in enumerate(totals):
        all_totals[:, 256 * at : 256 * at + 256] = part
    back_of(
        spans_b, weight_t, q_rows_b, v_rows_b, k_t_b, mixed_t_b, inverse_b, grad_b, probs_b, tokens_b, q_grad, k_grad, v_grad,
        *scratch,
    )
    totals, bias_rows = joint_totals(place, own_b, received_b, x_rows, q_grad, k_grad, v_grad)
    pack_totals([part + all_totals[:, 256 * at : 256 * at + 256] for at, part in enumerate(totals)], first_bias + bias_rows, choice, packed)


def back_of(
    spans, weight_t, q_rows, v_rows, k_t, mixed_t, inverse, mixed_grad_t, probs_far, tokens_grad, q_grad, k_grad, v_grad,
    q_grad_t, grad_rows, grad_t, extra_rows, probs_t, sems,
):
    def copies(tile, go):
        slot = lax.rem(tile, 2)
        for other in range(SEQ // TILE):

            @pl.when(met(spans, tile, other))
            def _():
                copy = pltpu.make_async_copy(
                    probs_far.at[other, tile], probs_t.at[slot, :, :, TILE * other : TILE * other + TILE], sems.at[slot, other]
                )
                copy.start() if go else copy.wait()

    copies(jnp.int32(0), True)
    scaled = []
    for head in range(6):
        rows = slice(32 * head, 32 * head + 32)
        part = mixed_grad_t[rows, :].astype(f32) * inverse[head : head + 1, :]
        delta = jnp.sum(part * mixed_t[rows, :].astype(f32), axis=0, keepdims=True)
        extra_rows[16 * head : 16 * head + 16, :] = three_terms(-delta)
        grad_t[rows, :] = part.astype(bf16)
        scaled.append(part)
    grad_rows[:, 0:PART] = jnp.transpose(jnp.concatenate(scaled, axis=0)).astype(bf16)
    grad_rows[:, PART:] = jnp.zeros((SEQ, 256 - PART), bf16)
    q_grad_t[...] = jnp.zeros_like(q_grad_t)

    def tile_of(tile, width, start):
        at = pl.ds(pl.multiple_of(tile * TILE, TILE), TILE)
        queries = pl.ds(pl.multiple_of(start * 128, 128), 128 * width)
        lane = lax.broadcasted_iota(jnp.int32, (128 * width, 256), 1)
        key_total = jnp.zeros((TILE, 256), f32)
        value_total = jnp.zeros((TILE, 256), f32)

        def spread(head):
            part = padded_head(
                grad_t[32 * head : 32 * head + 32, queries], head, 128 * width, extra_rows[16 * head : 16 * head + 16, queries]
            )
            return dot(v_rows[at, :], part)

        ahead = [spread(0)]
        for head in range(6):
            rows = slice(32 * head, 32 * head + 32)
            inside = (lane >= 32 * head) & (lane < 32 * head + 32)
            if head < 5:
                ahead.append(spread(head + 1))
            probs = probs_t[lax.rem(tile, 2), head, :, queries]
            scores_grad = probs * ahead[head].astype(bf16)
            one, other = q_rows[queries, :], grad_rows[queries, :]
            key_total += dot(scores_grad, jnp.where(inside, one, jnp.zeros_like(one)))
            value_total += dot(probs, jnp.where(inside, other, jnp.zeros_like(other)))
            q_grad_t[rows, queries] += dot(k_t[rows, at], scores_grad)
        k_grad[at, :] = (key_total * (1.0 / LOG2E)).astype(bf16)
        v_grad[at, :] = value_total.astype(bf16)

    def step(tile, carried):
        @pl.when(tile + 1 < SEQ // TILE)
        def _():
            copies(tile + 1, True)

        copies(tile, False)
        for width in WIDTHS:

            @pl.when(spans[1, tile] == width)
            def _():
                tile_of(tile, width, spans[0, tile])

        return carried

    lax.fori_loop(0, SEQ // TILE, step, 0)
    q_grad[:, 0:PART] = jnp.transpose(q_grad_t[...] * SCALE).astype(bf16)
    q_grad[:, PART:] = jnp.zeros((SEQ, 256 - PART), bf16)
    tokens_grad[...] = (
        dot(q_grad[:, 0:PART], weight_t[0:PART, :])
        + dot(k_grad[:, 0:PART], weight_t[256 : 256 + PART, :])
        + dot(v_grad[:, 0:PART], weight_t[512 : 512 + PART, :])
    ).astype(bf16)


def joint_totals(place, own, received, x_rows, q_grad, k_grad, v_grad):
    for half, block in ((place[0], own), (1 - place[0], received)):
        x_rows[pl.ds(pl.multiple_of(half * HALF, HALF), HALF), :] = block[...]
    totals = [dot_tn(x_rows[...], part[...]) for part in (q_grad, k_grad, v_grad)]
    bias_rows = jnp.concatenate(
        [jnp.sum(part[...].astype(f32), axis=0, keepdims=True) for part in (q_grad, v_grad)] + [jnp.zeros((6, 256), f32)],
        axis=0,
    )
    return totals, bias_rows


def pack_totals(totals, bias_rows, choice, packed):
    q_all, k_all, v_all = totals
    low_lanes = lax.broadcasted_iota(jnp.int32, (D, 128), 1) < 64
    fourth = jnp.where(low_lanes, q_all[:, 128:], pltpu.roll(k_all[:, 128:], 64, 1))
    fifth = jnp.where(low_lanes, v_all[:, 128:], 0.0)
    ends = jnp.where(low_lanes[:8], 0.0, pltpu.roll(bias_rows[:, 128:], 64, 1))
    biases = jnp.concatenate([bias_rows[0:2, 0:128], ends[0:2], jnp.zeros((12, 128), f32)], axis=0)
    for step_at in range(8):
        rows = slice(48 * step_at, 48 * step_at + 48)
        stacked = jnp.concatenate(
            [q_all[rows, 0:128], k_all[rows, 0:128], v_all[rows, 0:128], fourth[rows], fifth[rows], biases], axis=0
        ).astype(bf16)
        packed[256 * step_at : 256 * step_at + 256, :] = dot(choice[...], stacked).astype(bf16)


def normal_parts(values):
    mean = jnp.mean(values, axis=-1, keepdims=True)
    centered = values - mean
    scale = lax.rsqrt(jnp.mean(centered * centered, axis=-1, keepdims=True) + 1e-05)
    return centered * scale, scale


def normal_back(cotangent, normal, scale, gain):
    weighted = cotangent * gain
    mean = jnp.mean(weighted, axis=-1, keepdims=True)
    along = jnp.mean(weighted * normal, axis=-1, keepdims=True)
    return scale * (weighted - mean - normal * along)


def column_sum(matrix):
    return jnp.sum(matrix.astype(f32), axis=0, keepdims=True)


def feed_forward(
    place, own, received, own_grad, received_grad, mixed_a, mixed_b, choice, choice_t,
    far_a, far_b,
    out_own, out_received, attn_own, attn_received, back_a, back_b, packed_keep, packed_send,
    proj, up, down, up_total, down_total_t, proj_total, activated, slope, pieces, sems,
):
    core, near = place[1], place[0]
    arrivals = [
        pltpu.make_async_copy(far, pieces.at[at], sems.at[at]) for at, far in enumerate((far_a, far_b))
    ]
    for arrival in arrivals:
        arrival.start()
    for arrival in arrivals:
        arrival.wait()
    vectors = jnp.zeros((16, D), f32)
    for step in range(8):
        rows = slice(256 * step, 256 * step + 256)
        out = dot(choice[core], pieces[0, rows, :]) + dot(choice[1 - core], pieces[1, rows, :])
        proj[48 * step : 48 * step + 48, :] = out[0:48].astype(bf16)
        for block in range(4):
            up[48 * step : 48 * step + 48, D * block : D * block + D] = out[48 + 48 * block : 96 + 48 * block].astype(bf16)
        down[192 * step : 192 * step + 192, :] = out[240:432].astype(bf16)
        vectors = vectors + out[432:448]
    proj_bias, first_gain, first_shift, down_bias, second_gain, second_shift = (vectors[i : i + 1] for i in range(6))
    up_bias = jnp.concatenate([vectors[i : i + 1] for i in range(6, 10)], axis=1)
    rows_a = pl.ds(pl.multiple_of(core * PART, PART), PART)
    rows_b = pl.ds(pl.multiple_of((1 - core) * PART, PART), PART)
    sums = None
    blocks = ((near, own, own_grad, out_own, attn_own), (1 - near, received, received_grad, out_received, attn_received))
    for number in range(SEQ // FFN_ROWS):
        half, block, grad_block, out_block, attn_block = blocks[number * FFN_ROWS // HALF]
        inside = number * FFN_ROWS % HALF
        here = slice(inside, inside + FFN_ROWS)
        at = pl.ds(pl.multiple_of(half * HALF + inside, FFN_ROWS), FFN_ROWS)
        heads_a, heads_b = mixed_a[:, at], mixed_b[:, at]
        residual = block[here, :].astype(f32) + (dot_tn(heads_a, proj[rows_a, :]) + dot_tn(heads_b, proj[rows_b, :]) + proj_bias)
        first_normal, first_scale = normal_parts(residual)
        first_norm = first_normal * first_gain + first_shift
        first_low = first_norm.astype(bf16)
        for col in range(4):
            cols = slice(D * col, D * col + D)
            hidden = dot(first_low, up[:, cols]) + up_bias[:, cols]
            bell = jnp.exp2(hidden * hidden * (-0.5 * LOG2E))
            inner = 1.0 / (1.0 + jnp.abs(hidden) * (0.3275911 / math.sqrt(2)))
            series = inner * (0.127414796 + inner * (-0.142248368 + inner * (0.7107068705 + inner * (-0.7265760135 + inner * 0.5307027145))))
            tail = series * bell
            below = jnp.where(hidden >= 0.0, 1.0 - tail, tail)
            activated[:, cols] = (hidden * below).astype(bf16)
            slope[:, cols] = below + hidden * bell * (1.0 / math.sqrt(2 * math.pi))
        second_sum = first_norm + (dot(activated[...], down[...]) + down_bias)
        second_normal, second_scale = normal_parts(second_sum)
        out_block[here, :] = (second_normal * second_gain + second_shift).astype(bf16)
        out_grad = grad_block[here, :].astype(f32)
        second_grad = normal_back(out_grad, second_normal, second_scale, second_gain)
        branch_grad = second_grad.astype(bf16)
        first_grad = second_grad
        up_bias_grads = []
        for col in range(4):
            cols = slice(D * col, D * col + D)
            up_grad = (dot_nt(branch_grad, down[cols, :]) * slope[:, cols]).astype(bf16)
            first_grad = first_grad + dot_nt(up_grad, up[:, cols])
            up_bias_grads.append(column_sum(up_grad))
            up_new = dot_tn(first_low, up_grad)
            down_new = dot_tn(branch_grad, activated[:, cols])
            if number == 0:
                up_total[:, cols] = up_new
                down_total_t[:, cols] = down_new
            else:
                up_total[:, cols] += up_new
                down_total_t[:, cols] += down_new
        residual_grad = normal_back(first_grad, first_normal, first_scale, first_gain)
        attn_grad = residual_grad.astype(bf16)
        attn_block[here, :] = attn_grad
        back_a[:, at] = dot_nt(proj[rows_a, :], attn_grad).astype(bf16)
        back_b[:, at] = dot_nt(proj[rows_b, :], attn_grad).astype(bf16)
        new_a, new_b = dot(heads_a, attn_grad), dot(heads_b, attn_grad)
        if number == 0:
            proj_total[rows_a, :] = new_a
            proj_total[rows_b, :] = new_b
        else:
            proj_total[rows_a, :] += new_a
            proj_total[rows_b, :] += new_b
        new = [
            column_sum(attn_grad),
            column_sum(first_grad * first_normal),
            column_sum(first_grad),
            column_sum(branch_grad),
            column_sum(out_grad * second_normal),
            column_sum(out_grad),
        ] + up_bias_grads
        sums = new if sums is None else [a + b for a, b in zip(sums, new)]
    vector_rows = jnp.concatenate(sums + [jnp.zeros((6, D), f32)], axis=0)
    for pair in range(4):
        down_rows = jnp.transpose(down_total_t[:, D * pair : D * pair + D])
        for inner_step in range(2):
            step = 2 * pair + inner_step
            rows = slice(48 * step, 48 * step + 48)
            stacked = jnp.concatenate(
                [proj_total[rows, :]]
                + [up_total[rows, D * block : D * block + D] for block in range(4)]
                + [down_rows[192 * inner_step : 192 * inner_step + 192], vector_rows],
                axis=0,
            ).astype(bf16)
            packed_rows = slice(256 * step, 256 * step + 256)
            packed_keep[packed_rows, :] = dot(choice_t[core], stacked).astype(bf16)
            packed_send[packed_rows, :] = dot(choice_t[1 - core], stacked).astype(bf16)


def finish(
    place, joint, joint_core, joint_near, joint_across, half, got,
    qkv, q_bias, v_bias, proj, proj_bias, first_gain, first_shift, up, up_bias, down, down_bias, second_gain, second_shift,
):
    rank = place[2]
    here = place[0] == place[1]
    mine = jnp.where(here, joint[...], joint_near[...])
    theirs = jnp.where(here, joint_core[...], joint_across[...])
    total = jnp.stack([jnp.where(place[1] == 0, mine, theirs), jnp.where(place[1] == 0, theirs, mine)])
    columns = []
    for first, tail_row, tail_lane in ((0, 18, 0), (6, 18, 64), (12, 24, 0)):
        for side in range(2):
            columns.append(total[side, first : first + 6, :])
            columns.append(total[side, tail_row : tail_row + 6, tail_lane : tail_lane + 64])
    qkv[...] = jnp.concatenate(columns, axis=1)
    low, high = half[...].astype(f32), got[...].astype(f32)
    first = place[0] == 0
    rest = jnp.concatenate([jnp.where(first, low, high), jnp.where(first, high, low)], axis=0)
    proj[...] = rest[0:6]
    up[...] = jnp.concatenate([rest[6 + 6 * block : 12 + 6 * block] for block in range(4)], axis=1)
    down[...] = rest[30:54]
    biases = [
        jnp.concatenate([total[0, row : row + 1], total[0, end : end + 1, 64:], total[1, row : row + 1], total[1, end : end + 1, 64:]], axis=1)
        for row, end in ((30, 24), (31, 25))
    ]
    vectors = jnp.concatenate(biases + [rest[54:60]], axis=0)
    vectors = pltpu.roll(vectors, lax.rem(D - ROWS * rank, D), 1)
    for at, out in enumerate((q_bias, v_bias, proj_bias, first_gain, first_shift, down_bias, second_gain, second_shift)):
        out[...] = vectors[at, 0:ROWS]
    long = jnp.concatenate([rest[60 + at : 61 + at] for at in range(4)], axis=1)
    long = pltpu.roll(jnp.concatenate([long] * 8, axis=0), lax.rem(FF - 24 * rank, FF), 1)
    up_bias[...] = long[0, 0:24]


def swap_core(value):
    return lax.ppermute(value, "c", SWAP)


def from_along(value, axis, step):
    return lax.ppermute(value, axis, tuple(((at + step) % 4, at) for at in range(4)))


def swap_ctx(value):
    return lax.ppermute(value, "zl", SWAP)


def spread_out(vector, rank):
    size = vector.shape[0]
    return lax.dynamic_update_slice(jnp.zeros((size * RANKS,), bf16), vector, (size * rank,))


def pack_joint(qkv_weight, query_bias, value_bias, rank):
    query_all, value_all = spread_out(query_bias, rank), spread_out(value_bias, rank)
    pieces = []
    for core in range(2):
        q, k, v = (qkv_weight[:, D * at + PART * core : D * at + PART * core + PART] for at in range(3))
        q_bias, v_bias = (part[PART * core : PART * core + PART] for part in (query_all, value_all))
        ends = jnp.concatenate([q_bias[None, 128:], v_bias[None, 128:], jnp.zeros((4, 64), bf16)], axis=0)
        pieces.append(
            jnp.concatenate(
                [
                    q[:, :128],
                    k[:, :128],
                    v[:, :128],
                    jnp.concatenate([q[:, 128:], k[:, 128:]], axis=1),
                    jnp.concatenate([v[:, 128:], ends], axis=1),
                    q_bias[None, :128],
                    v_bias[None, :128],
                ],
                axis=0,
            )
        )
    return jnp.stack(pieces)


def pack_rest(proj_weight, up_weight, down_weight, vectors, up_bias, rank):
    return jnp.concatenate(
        [proj_weight]
        + [up_weight[:, D * block : D * block + D] for block in range(4)]
        + [down_weight]
        + [spread_out(vector, rank)[None] for vector in vectors]
        + [spread_out(up_bias, rank).reshape(4, D)],
        axis=0,
    )


def spans_of(ids):
    first, last = ids[0, 0::TILE], ids[0, TILE - 1 :: TILE]
    low = jnp.sum(ids < first[:, None], axis=1, dtype=jnp.int32) // 128
    high = (jnp.sum(ids <= last[:, None], axis=1, dtype=jnp.int32) + 127) // 128
    needed = high - low
    width = jnp.where(needed <= WIDTHS[0], WIDTHS[0], jnp.where(needed <= WIDTHS[1], WIDTHS[1], WIDTHS[2]))
    return jnp.stack([jnp.minimum(low, 8 - width), width])


def local(
    tokens, segment_ids, out_grad, qkv_weight, query_bias, value_bias, proj_weight, proj_bias, first_gain, first_shift,
    up_weight, up_bias, down_weight, down_bias, second_gain, second_shift,
):
    x, y, zh, core, near = (lax.axis_index(name) for name in ALL)
    rank = ((x * 4 + y) * 2 + zh) * 2 + core
    groups = RANKS // 2
    place = jnp.stack([near, core, rank, x, y, zh]).astype(jnp.int32)
    take = functools.partial(lax.dynamic_index_in_dim, axis=0, keepdims=False)

    piece = pack_joint(qkv_weight, query_bias, value_bias, rank)
    piece = lax.dynamic_slice_in_dim(piece, 16 * near, 16, axis=1)
    sent = jnp.broadcast_to(piece[None, :, None], (groups, 2, 2, 16, 128)).reshape(4 * groups, 16, 128)
    joint_packed = lax.all_to_all(sent, ALL, 0, 0, tiled=True).reshape(groups * 64, 128)

    own = take(tokens, near)
    received = swap_ctx(take(tokens, 1 - near))
    ids_own = take(segment_ids, near)
    ids_received = swap_ctx(take(segment_ids, 1 - near))
    ids = jnp.where(near == 0, jnp.concatenate([ids_own, ids_received]), jnp.concatenate([ids_received, ids_own]))[None]
    ids_other = swap_core(ids)
    own_other, received_other = swap_core(own), swap_core(received)
    grad_own = take(out_grad, near)
    grad_sent = take(out_grad, 1 - near)

    piece = pack_rest(
        proj_weight, up_weight, down_weight,
        (proj_bias, first_gain, first_shift, down_bias, second_gain, second_shift), up_bias, rank,
    )
    piece = lax.dynamic_slice_in_dim(piece, 32 * near, 32, axis=0)
    sent = jnp.broadcast_to(piece[None], (2 * groups, 32, D))
    sent, grad_sent, joint_packed, received, received_other, own_other, ids_other = lax.optimization_barrier(
        (sent, grad_sent, joint_packed, received, received_other, own_other, ids_other)
    )
    packed_a = lax.all_to_all(sent, ("x", "y", "zh", "zl"), 0, 0, tiled=True).reshape(groups * 64, D)
    spans, spans_other = spans_of(ids), spans_of(ids_other)
    ids_other, ids = ids_other.astype(f32), ids.astype(f32)

    choice = joint_choice()
    weight, weight_t, bias, bias_t = call(
        unpack_joint, 2, [((D, 768), bf16), ((768, D), bf16), ((8, 256), f32), ((256, 128), f32)], name="unpack"
    )(joint_packed, jnp.asarray(choice, bf16))

    tiles = SEQ // TILE
    attention = call(
        attend,
        7,
        [
            ((SEQ, 256), bf16), ((SEQ, 256), bf16), ((PART, SEQ), bf16), ((PART, SEQ), bf16), ((8, SEQ), f32),
            ((tiles, tiles, 6, TILE, TILE), bf16),
        ],
        scratch=[
            pltpu.VMEM((PART, SEQ), bf16), pltpu.VMEM((SEQ, 256), bf16), pltpu.VMEM((PART + 16, SEQ), bf16),
            pltpu.VMEM((SEQ, 128), f32), pltpu.VMEM((2, 6, SEQ, TILE), bf16), pltpu.SemaphoreType.DMA((2, tiles)),
        ],
        scalars=2,
        flops=8 * 10**9,
        name="attend",
        far_outs=1,
    )
    *kept_other, probs_other = attention(
        place, spans_other, own_other, received_other, weight, weight_t, bias, bias_t, ids_other
    )
    mixed_other, own, packed_a = lax.optimization_barrier((kept_other[3], own, packed_a))
    mixed_b = swap_core(mixed_other)
    packed_b = swap_core(packed_a)
    grad_received = swap_ctx(grad_sent)
    *kept, probs = attention(place, spans, own, received, weight, weight_t, bias, bias_t, ids)
    mixed_a = kept[3]

    out_own, out_received, attn_own, attn_received, back_a, back_b, packed_keep, packed_send = call(
        feed_forward,
        10,
        [((HALF, D), bf16)] * 4 + [((PART, SEQ), bf16)] * 2 + [((2048, D), bf16)] * 2,
        scratch=[
            pltpu.VMEM((D, D), bf16), pltpu.VMEM((D, FF), bf16), pltpu.VMEM((FF, D), bf16), pltpu.VMEM((D, FF), f32),
            pltpu.VMEM((D, FF), f32), pltpu.VMEM((D, D), f32), pltpu.VMEM((FFN_ROWS, FF), bf16),
            pltpu.VMEM((FFN_ROWS, FF), f32), pltpu.VMEM((2, 2048, D), bf16), pltpu.SemaphoreType.DMA((2,)),
        ],
        scalars=1,
        flops=10 * 10**9,
        name="feed_forward",
        far_ins=2,
    )(
        place, own, received, grad_own, grad_received, mixed_a, mixed_b,
        jnp.asarray(rest_choice(), bf16), jnp.asarray(rest_choice().transpose(0, 2, 1), bf16), packed_a, packed_b,
    )

    back_other = swap_core(back_b)
    packed_got = swap_core(packed_send)
    rest_sum = (packed_keep.astype(f32) + packed_got.astype(f32)).astype(bf16).reshape(2 * groups, 32, D)
    rest_sum, back_other, back_a, out_received = lax.optimization_barrier((rest_sum, back_other, back_a, out_received))
    out_back = swap_ctx(out_received)
    rest_all = lax.all_to_all(rest_sum, ("x", "y", "zh", "zl"), 0, 0, tiled=True)

    back_scratch = [
        pltpu.VMEM((PART, SEQ), f32), pltpu.VMEM((SEQ, 256), bf16), pltpu.VMEM((PART, SEQ), bf16),
        pltpu.VMEM((96, SEQ), bf16), pltpu.VMEM((2, 6, TILE, SEQ), bf16), pltpu.SemaphoreType.DMA((2, tiles)),
    ]
    rows = ((SEQ, 256), bf16)
    partial, partial_other, joint_sent = call(
        attend_back,
        20,
        [((SEQ, D), bf16), ((SEQ, D), bf16), ((2048, 128), bf16)],
        scratch=[pltpu.VMEM(*rows)] * 3 + [pltpu.VMEM((SEQ, D), bf16), pltpu.VMEM((D, 768), f32)] + back_scratch,
        scalars=3,
        flops=40 * 10**9,
        name="attend_back",
        far_ins=2,
    )(
        place, spans, spans_other, own, received, weight_t, *kept, back_a, *kept_other, back_other, own_other, received_other,
        jnp.asarray(choice.T, bf16), probs, probs_other,
    )
    joint_sent, partial_other, rest_all, out_back = lax.optimization_barrier((joint_sent, partial_other, rest_all, out_back))

    partial_got = swap_core(partial_other)
    rest_half = jnp.sum(rest_all.astype(f32), axis=0).astype(bf16)
    whole = partial.astype(f32) + partial_got.astype(f32)
    mine = lax.dynamic_slice_in_dim(whole, HALF * near, HALF, axis=0) + attn_own.astype(f32)
    theirs = lax.dynamic_slice_in_dim(whole, HALF * (1 - near), HALF, axis=0) + attn_received.astype(f32)
    mine, theirs = mine.astype(bf16), theirs.astype(bf16)
    tokens_back, rest_got = swap_ctx(theirs), swap_ctx(rest_half)
    def ordered(kept_part, got_part):
        return jnp.where(near == 0, jnp.stack([kept_part, got_part]), jnp.stack([got_part, kept_part]))

    joint_all = lax.all_to_all(joint_sent.reshape(RANKS, 32, 128), ("x", "y", "zh", "zl"), 0, 0, tiled=True)
    joint_sum = jnp.sum(joint_all.astype(f32), axis=0)
    joint_parts = [
        joint_sum,
        swap_core(joint_sum),
        swap_ctx(joint_sum),
        lax.ppermute(joint_sum, ("c", "zl"), ((0, 3), (3, 0), (1, 2), (2, 1))),
    ]
    vector = ((ROWS,), f32)
    grads = call(
        finish,
        6,
        [
            ((ROWS, 3 * D), f32), vector, vector, ((ROWS, D), f32), vector, vector, vector, ((ROWS, FF), f32),
            ((24,), f32), ((24, D), f32), vector, vector, vector,
        ],
        scalars=1,
        name="finish",
        limit=16,
    )(place, *joint_parts, rest_half, rest_got)
    return (ordered(out_own, out_back), ordered(mine, tokens_back), *grads)


def solution(mesh):
    grid = Mesh(mesh.devices.reshape(4, 4, 2, 2, 2), ALL)
    ranks = ("x", "y", "zh", "c")
    data, matrix, vector = P(ranks, "zl", None), P(ranks, None), P(ranks)
    in_specs = (
        data, P(ranks, "zl"), data, matrix, vector, vector, matrix, vector, vector, vector, matrix, vector, matrix,
        vector, vector, vector,
    )
    out_specs = (
        data, data, matrix, vector, vector, matrix, vector, vector, vector, matrix, vector, matrix, vector, vector,
        vector,
    )
    return jax.shard_map(local, mesh=grid, in_specs=in_specs, out_specs=out_specs, check_vma=False)
```

```python
import functools
import math

import jax
import jax.numpy as jnp
import numpy as np
from jax import lax
from jax.experimental import pallas as pl
from jax.experimental.pallas import tpu as pltpu
from jax.sharding import Mesh
from jax.sharding import PartitionSpec as P

D = 384
FF = 1536
SEQ = 1024
HALF = 512
PART = 192
RANKS = 64
ROWS = D // RANKS
SCALE = 1.0 / math.sqrt(32)
LOG2E = math.log2(math.e)
BOUND = 60.0
TILE = 256
FFN_ROWS = 512
WIDTHS = (3, 5, 8)

bf16 = jnp.bfloat16
f32 = jnp.float32
VMEM = pl.BlockSpec(memory_space=pltpu.VMEM)
SMEM = pl.BlockSpec(memory_space=pltpu.SMEM)
FAR = pl.BlockSpec(memory_space=pl.ANY)
SWAP = ((0, 1), (1, 0))
ALL = ("x", "y", "zh", "c", "zl")


def dot(left, right):
    return lax.dot_general(left, right, (((1,), (0,)), ((), ())), preferred_element_type=f32)


def dot_nt(left, right):
    return lax.dot_general(left, right, (((1,), (1,)), ((), ())), preferred_element_type=f32)


def dot_tn(left, right):
    return lax.dot_general(left, right, (((0,), (0,)), ((), ())), preferred_element_type=f32)


def joint_choice():
    choice = np.zeros((256, 256), np.float32)
    for rank in range(8):
        for block in range(5):
            for row in range(ROWS):
                choice[48 * block + ROWS * rank + row, 32 * rank + ROWS * block + row] = 1
        for place, row in ((240, 30), (241, 31), (242, 24), (243, 25)):
            choice[place, 32 * rank + row] = 1
    return choice


def rest_choice():
    choice = np.zeros((2, 448, 256), np.float32)
    for core in range(2):
        for at in range(4):
            rank = 2 * at + core
            for row in range(ROWS):
                for block in range(5):
                    choice[core, 48 * block + ROWS * rank + row, 64 * at + ROWS * block + row] = 1
            for row in range(24):
                choice[core, 240 + 24 * rank + row, 64 * at + 30 + row] = 1
            for row in range(10):
                choice[core, 432 + row, 64 * at + 54 + row] = 1
    return choice


def call(kernel, ins, outs, scratch=(), scalars=0, flops=0, name=None, far_ins=0, far_outs=0, limit=56, near=()):
    return pl.pallas_call(
        kernel,
        in_specs=[SMEM] * scalars + [VMEM] * (ins - far_ins) + [FAR] * far_ins,
        out_specs=[VMEM] * (len(outs) - far_outs) + [FAR] * far_outs,
        out_shape=[
            pltpu.VMEM(shape, dtype) if at in near else jax.ShapeDtypeStruct(shape, dtype)
            for at, (shape, dtype) in enumerate(outs)
        ],
        scratch_shapes=scratch,
        compiler_params=pltpu.CompilerParams(vmem_limit_bytes=limit * 2**20),
        cost_estimate=pl.CostEstimate(flops=flops, bytes_accessed=4 * 2**20, transcendentals=0),
        name=name,
    )


def keep_near(value):
    return pltpu.with_memory_space_constraint(value, pltpu.VMEM)


def unpack_joint(packed, choice, weight, weight_t, bias, bias_t):
    low_lanes = lax.broadcasted_iota(jnp.int32, (48, 128), 1) < 64
    total = jnp.zeros((16, 128), f32)
    for step in range(8):
        out = dot(choice[...], packed[256 * step : 256 * step + 256, :])
        rows = slice(48 * step, 48 * step + 48)
        mixed = out[144:192]
        weight[rows, 0:128] = out[0:48].astype(bf16)
        weight[rows, 256:384] = out[48:96].astype(bf16)
        weight[rows, 512:640] = out[96:144].astype(bf16)
        weight[rows, 128:256] = jnp.where(low_lanes, mixed, 0.0).astype(bf16)
        weight[rows, 384:512] = jnp.where(low_lanes, pltpu.roll(mixed, 64, 1), 0.0).astype(bf16)
        weight[rows, 640:768] = jnp.where(low_lanes, out[192:240], 0.0).astype(bf16)
        total = total + out[240:256]
    tail = jnp.where(low_lanes[:16], pltpu.roll(total, 64, 1), 0.0)
    both = jnp.concatenate([total[0:2], jnp.zeros((6, 128), f32)], axis=0)
    tails = jnp.concatenate([tail[2:4], jnp.zeros((6, 128), f32)], axis=0)
    rows = jnp.concatenate([both, tails], axis=1)
    bias[...] = rows
    bias_t[...] = jnp.transpose(jnp.concatenate([rows, jnp.zeros((120, 256), f32)], axis=0))
    weight_t[...] = jnp.transpose(weight[...].astype(f32)).astype(bf16)


def padded_head(matrix, head, lanes, extra=None):
    parts = []
    if head:
        parts.append(jnp.zeros((32 * head, lanes), bf16))
    parts.append(matrix)
    if extra is None:
        parts.append(jnp.zeros((224 - 32 * head, lanes), bf16))
    else:
        if head < 5:
            parts.append(jnp.zeros((160 - 32 * head, lanes), bf16))
        parts.append(extra)
        parts.append(jnp.zeros((48, lanes), bf16))
    return jnp.concatenate(parts, axis=0)


def id_columns(id_row):
    return jnp.transpose(jnp.broadcast_to(id_row, (128, SEQ)))


def met(spans, one, other):
    def reached(tile, by):
        return (2 * tile + 1 >= spans[0, by]) & (2 * tile < spans[0, by] + spans[1, by])

    return reached(one, other) | reached(other, one)


def attend(
    place, spans_a, spans_b, own_a, received_a, own_b, received_b, weight, weight_t, bias, bias_t, id_row_a, id_row_b,
    q_rows_a, v_rows_a, k_t_a, mixed_t_a, inverse_a, q_rows_b, v_rows_b, k_t_b, mixed_t_b, inverse_b, probs_a, probs_b, *scratch,
):
    shared = (weight, weight_t, bias, bias_t)
    left = attend_to(
        place, spans_b, own_b, received_b, *shared, id_row_b, q_rows_b, v_rows_b, k_t_b, mixed_t_b, inverse_b, probs_b, None,
        *scratch,
    )
    left = attend_to(
        place, spans_a, own_a, received_a, *shared, id_row_a, q_rows_a, v_rows_a, k_t_a, mixed_t_a, inverse_a, probs_a, left,
        *scratch,
    )
    left()


def attend_to(
    place, spans, own, received, weight, weight_t, bias, bias_t, id_row,
    q_rows, v_rows, k_t, mixed_t, inverse, probs_far, before, q_t, k_rows, v_t, ids_t, probs_t, sems,
):
    lane = lax.broadcasted_iota(jnp.int32, (HALF, 256), 1) < PART
    for half, block in ((place[0], own), (1 - place[0], received)):
        at = pl.ds(pl.multiple_of(half * HALF, HALF), HALF)
        tokens = block[...]
        flat = dot(tokens, weight[...])
        q_rows[at, :] = ((flat[:, 0:256] + bias[0:1, :]) * (SCALE * LOG2E)).astype(bf16)
        k_rows[at, :] = flat[:, 256:512].astype(bf16)
        v_rows[at, :] = jnp.where(lane, flat[:, 512:768] + bias[1:2, :], 1.0).astype(bf16)
        q_t[:, at] = ((dot_nt(weight_t[0:PART, :], tokens) + bias_t[0:PART, 0:1]) * (SCALE * LOG2E)).astype(bf16)
        k_t[:, at] = dot_nt(weight_t[256 : 256 + PART, :], tokens).astype(bf16)
        v_t[0:PART, at] = (dot_nt(weight_t[512 : 512 + PART, :], tokens) + bias_t[0:PART, 1:2]).astype(bf16)
    v_t[PART:, :] = jnp.ones((16, SEQ), bf16)
    ids_t[...] = id_columns(id_row[...])
    inverse[...] = jnp.ones_like(inverse)
    largest = jnp.zeros((), f32)
    for head in range(6):
        rows = slice(32 * head, 32 * head + 32)
        q_size = jnp.max(jnp.sum(jnp.square(q_t[rows, :].astype(f32)), axis=0, keepdims=True))
        k_size = jnp.max(jnp.sum(jnp.square(k_t[rows, :].astype(f32)), axis=0, keepdims=True))
        largest = jnp.maximum(largest, q_size * k_size)
    small = largest <= BOUND * BOUND

    def tile_of(tile, width, start, shift):
        at = pl.ds(pl.multiple_of(tile * TILE, TILE), TILE)
        keys = pl.ds(pl.multiple_of(start * 128, 128), 128 * width)
        slot = lax.rem(tile, 2)
        if width < 8:
            for block in range(8):

                @pl.when((block < start) | (block >= start + width))
                def _():
                    probs_t[slot, :, 128 * block : 128 * block + 128, :] = jnp.zeros((6, 128, TILE), bf16)

        same = jnp.concatenate([ids_t[keys, :]] * 2, axis=1) == id_row[:, at]
        keep = same.astype(f32).astype(bf16)

        def score(head):
            return dot(k_rows[keys, :], padded_head(q_t[32 * head : 32 * head + 32, at], head, TILE))

        ahead = [score(0)]
        for head in range(6):
            rows = slice(32 * head, 32 * head + 32)
            if head < 5:
                ahead.append(score(head + 1))
            scores = ahead[head]
            if shift:
                scores = jnp.where(same, scores, -1e30)
                probs = jnp.exp2(scores - jnp.max(scores, axis=0, keepdims=True)).astype(bf16)
            else:
                probs = jnp.exp2(scores).astype(bf16) * keep
            probs_t[slot, head, keys, :] = probs
            mixed = dot(jnp.concatenate([v_t[rows, keys], v_t[PART:, keys]], axis=0), probs)
            over = 1.0 / mixed[32:33]
            mixed_t[rows, at] = (mixed[0:32] * over).astype(bf16)
            inverse[head : head + 1, at] = over

    def copies(tile, go):
        slot = lax.rem(tile, 2)
        for other in range(SEQ // TILE):

            @pl.when(met(spans, tile, other))
            def _():
                copy = pltpu.make_async_copy(
                    probs_t.at[slot, :, TILE * other : TILE * other + TILE, :], probs_far.at[tile, other], sems.at[slot, other]
                )
                copy.start() if go else copy.wait()

    def step(tile, carried):
        @pl.when(tile >= 2)
        def _():
            copies(tile - 2, False)

        for width in WIDTHS:

            @pl.when(small & (spans[1, tile] == width))
            def _():
                tile_of(tile, width, spans[0, tile], False)

        @pl.when(jnp.logical_not(small))
        def _():
            tile_of(tile, 8, 0, True)

        copies(tile, True)
        return carried

    if before is not None:
        before()
    lax.fori_loop(0, SEQ // TILE, step, 0)

    def left():
        for tile in range(SEQ // TILE - 2, SEQ // TILE):
            copies(tile, False)

    return left


def three_terms(row):
    first = row.astype(bf16).astype(f32)
    second = (row - first).astype(bf16).astype(f32)
    third = row - first - second
    return jnp.concatenate([first, second, third, jnp.zeros((13, row.shape[1]), f32)], axis=0).astype(bf16)


def attend_back(
    place, spans_a, spans_b, own, received, weight_t,
    q_rows_a, v_rows_a, k_t_a, mixed_t_a, inverse_a, grad_a, q_rows_b, v_rows_b, k_t_b, mixed_t_b, inverse_b, grad_b,
    own_b, received_b, choice, probs_a, probs_b, tokens_a, tokens_b, packed, q_grad, k_grad, v_grad, x_rows, all_totals, *scratch,
):
    back_of(
        spans_a, weight_t, q_rows_a, v_rows_a, k_t_a, mixed_t_a, inverse_a, grad_a, probs_a, tokens_a, q_grad, k_grad, v_grad,
        *scratch,
    )
    totals, first_bias = joint_totals(place, own, received, x_rows, q_grad, k_grad, v_grad)
    for at, part in enumerate(totals):
        all_totals[:, 256 * at : 256 * at + 256] = part
    back_of(
        spans_b, weight_t, q_rows_b, v_rows_b, k_t_b, mixed_t_b, inverse_b, grad_b, probs_b, tokens_b, q_grad, k_grad, v_grad,
        *scratch,
    )
    totals, bias_rows = joint_totals(place, own_b, received_b, x_rows, q_grad, k_grad, v_grad)
    pack_totals([part + all_totals[:, 256 * at : 256 * at + 256] for at, part in enumerate(totals)], first_bias + bias_rows, choice, packed)


def back_of(
    spans, weight_t, q_rows, v_rows, k_t, mixed_t, inverse, mixed_grad_t, probs_far, tokens_grad, q_grad, k_grad, v_grad,
    q_grad_t, grad_rows, grad_t, extra_rows, probs_t, sems,
):
    def copies(tile, go):
        slot = lax.rem(tile, 2)
        for other in range(SEQ // TILE):

            @pl.when(met(spans, tile, other))
            def _():
                copy = pltpu.make_async_copy(
                    probs_far.at[other, tile], probs_t.at[slot, :, :, TILE * other : TILE * other + TILE], sems.at[slot, other]
                )
                copy.start() if go else copy.wait()

    copies(jnp.int32(0), True)
    scaled = []
    for head in range(6):
        rows = slice(32 * head, 32 * head + 32)
        part = mixed_grad_t[rows, :].astype(f32) * inverse[head : head + 1, :]
        delta = jnp.sum(part * mixed_t[rows, :].astype(f32), axis=0, keepdims=True)
        extra_rows[16 * head : 16 * head + 16, :] = three_terms(-delta)
        grad_t[rows, :] = part.astype(bf16)
        scaled.append(part)
    grad_rows[:, 0:PART] = jnp.transpose(jnp.concatenate(scaled, axis=0)).astype(bf16)
    grad_rows[:, PART:] = jnp.zeros((SEQ, 256 - PART), bf16)
    q_grad_t[...] = jnp.zeros_like(q_grad_t)

    def tile_of(tile, width, start):
        at = pl.ds(pl.multiple_of(tile * TILE, TILE), TILE)
        queries = pl.ds(pl.multiple_of(start * 128, 128), 128 * width)
        lane = lax.broadcasted_iota(jnp.int32, (128 * width, 256), 1)
        key_total = jnp.zeros((TILE, 256), f32)
        value_total = jnp.zeros((TILE, 256), f32)

        def spread(head):
            part = padded_head(
                grad_t[32 * head : 32 * head + 32, queries], head, 128 * width, extra_rows[16 * head : 16 * head + 16, queries]
            )
            return dot(v_rows[at, :], part)

        ahead = [spread(0)]
        for head in range(6):
            rows = slice(32 * head, 32 * head + 32)
            inside = (lane >= 32 * head) & (lane < 32 * head + 32)
            if head < 5:
                ahead.append(spread(head + 1))
            probs = probs_t[lax.rem(tile, 2), head, :, queries]
            scores_grad = probs * ahead[head].astype(bf16)
            one, other = q_rows[queries, :], grad_rows[queries, :]
            key_total += dot(scores_grad, jnp.where(inside, one, jnp.zeros_like(one)))
            value_total += dot(probs, jnp.where(inside, other, jnp.zeros_like(other)))
            q_grad_t[rows, queries] += dot(k_t[rows, at], scores_grad)
        k_grad[at, :] = (key_total * (1.0 / LOG2E)).astype(bf16)
        v_grad[at, :] = value_total.astype(bf16)

    def step(tile, carried):
        @pl.when(tile + 1 < SEQ // TILE)
        def _():
            copies(tile + 1, True)

        copies(tile, False)
        for width in WIDTHS:

            @pl.when(spans[1, tile] == width)
            def _():
                tile_of(tile, width, spans[0, tile])

        return carried

    lax.fori_loop(0, SEQ // TILE, step, 0)
    q_grad[:, 0:PART] = jnp.transpose(q_grad_t[...] * SCALE).astype(bf16)
    q_grad[:, PART:] = jnp.zeros((SEQ, 256 - PART), bf16)
    tokens_grad[...] = (
        dot(q_grad[:, 0:PART], weight_t[0:PART, :])
        + dot(k_grad[:, 0:PART], weight_t[256 : 256 + PART, :])
        + dot(v_grad[:, 0:PART], weight_t[512 : 512 + PART, :])
    ).astype(bf16)


def joint_totals(place, own, received, x_rows, q_grad, k_grad, v_grad):
    for half, block in ((place[0], own), (1 - place[0], received)):
        x_rows[pl.ds(pl.multiple_of(half * HALF, HALF), HALF), :] = block[...]
    totals = [dot_tn(x_rows[...], part[...]) for part in (q_grad, k_grad, v_grad)]
    bias_rows = jnp.concatenate(
        [jnp.sum(part[...].astype(f32), axis=0, keepdims=True) for part in (q_grad, v_grad)] + [jnp.zeros((6, 256), f32)],
        axis=0,
    )
    return totals, bias_rows


def pack_totals(totals, bias_rows, choice, packed):
    q_all, k_all, v_all = totals
    low_lanes = lax.broadcasted_iota(jnp.int32, (D, 128), 1) < 64
    fourth = jnp.where(low_lanes, q_all[:, 128:], pltpu.roll(k_all[:, 128:], 64, 1))
    fifth = jnp.where(low_lanes, v_all[:, 128:], 0.0)
    ends = jnp.where(low_lanes[:8], 0.0, pltpu.roll(bias_rows[:, 128:], 64, 1))
    biases = jnp.concatenate([bias_rows[0:2, 0:128], ends[0:2], jnp.zeros((12, 128), f32)], axis=0)
    for step_at in range(8):
        rows = slice(48 * step_at, 48 * step_at + 48)
        stacked = jnp.concatenate(
            [q_all[rows, 0:128], k_all[rows, 0:128], v_all[rows, 0:128], fourth[rows], fifth[rows], biases], axis=0
        ).astype(bf16)
        packed[256 * step_at : 256 * step_at + 256, :] = dot(choice[...], stacked).astype(bf16)


def normal_parts(values):
    mean = jnp.mean(values, axis=-1, keepdims=True)
    centered = values - mean
    scale = lax.rsqrt(jnp.mean(centered * centered, axis=-1, keepdims=True) + 1e-05)
    return centered * scale, scale


def normal_back(cotangent, normal, scale, gain):
    weighted = cotangent * gain
    mean = jnp.mean(weighted, axis=-1, keepdims=True)
    along = jnp.mean(weighted * normal, axis=-1, keepdims=True)
    return scale * (weighted - mean - normal * along)


def column_sum(matrix):
    return jnp.sum(matrix.astype(f32), axis=0, keepdims=True)


def feed_forward(
    place, own, received, own_grad, received_grad, mixed_a, mixed_b, choice, choice_t,
    packed_a, packed_b,
    out_own, out_received, attn_own, attn_received, back_a, back_b, packed_keep, packed_send,
    proj, up, down, up_total, down_total_t, proj_total, activated, slope,
):
    core, near = place[1], place[0]
    vectors = jnp.zeros((16, D), f32)
    for step in range(8):
        rows = slice(256 * step, 256 * step + 256)
        out = dot(choice[core], packed_a[rows, :]) + dot(choice[1 - core], packed_b[rows, :])
        proj[48 * step : 48 * step + 48, :] = out[0:48].astype(bf16)
        for block in range(4):
            up[48 * step : 48 * step + 48, D * block : D * block + D] = out[48 + 48 * block : 96 + 48 * block].astype(bf16)
        down[192 * step : 192 * step + 192, :] = out[240:432].astype(bf16)
        vectors = vectors + out[432:448]
    proj_bias, first_gain, first_shift, down_bias, second_gain, second_shift = (vectors[i : i + 1] for i in range(6))
    up_bias = jnp.concatenate([vectors[i : i + 1] for i in range(6, 10)], axis=1)
    rows_a = pl.ds(pl.multiple_of(core * PART, PART), PART)
    rows_b = pl.ds(pl.multiple_of((1 - core) * PART, PART), PART)
    sums = None
    blocks = ((near, own, own_grad, out_own, attn_own), (1 - near, received, received_grad, out_received, attn_received))
    for number in range(SEQ // FFN_ROWS):
        half, block, grad_block, out_block, attn_block = blocks[number * FFN_ROWS // HALF]
        inside = number * FFN_ROWS % HALF
        here = slice(inside, inside + FFN_ROWS)
        at = pl.ds(pl.multiple_of(half * HALF + inside, FFN_ROWS), FFN_ROWS)
        heads_a, heads_b = mixed_a[:, at], mixed_b[:, at]
        residual = block[here, :].astype(f32) + (dot_tn(heads_a, proj[rows_a, :]) + dot_tn(heads_b, proj[rows_b, :]) + proj_bias)
        first_normal, first_scale = normal_parts(residual)
        first_norm = first_normal * first_gain + first_shift
        first_low = first_norm.astype(bf16)
        for col in range(4):
            cols = slice(D * col, D * col + D)
            hidden = dot(first_low, up[:, cols]) + up_bias[:, cols]
            bell = jnp.exp2(hidden * hidden * (-0.5 * LOG2E))
            inner = 1.0 / (1.0 + jnp.abs(hidden) * (0.3275911 / math.sqrt(2)))
            series = inner * (0.127414796 + inner * (-0.142248368 + inner * (0.7107068705 + inner * (-0.7265760135 + inner * 0.5307027145))))
            tail = series * bell
            below = jnp.where(hidden >= 0.0, 1.0 - tail, tail)
            activated[:, cols] = (hidden * below).astype(bf16)
            slope[:, cols] = below + hidden * bell * (1.0 / math.sqrt(2 * math.pi))
        second_sum = first_norm + (dot(activated[...], down[...]) + down_bias)
        second_normal, second_scale = normal_parts(second_sum)
        out_block[here, :] = (second_normal * second_gain + second_shift).astype(bf16)
        out_grad = grad_block[here, :].astype(f32)
        second_grad = normal_back(out_grad, second_normal, second_scale, second_gain)
        branch_grad = second_grad.astype(bf16)
        first_grad = second_grad
        up_bias_grads = []
        for col in range(4):
            cols = slice(D * col, D * col + D)
            up_grad = (dot_nt(branch_grad, down[cols, :]) * slope[:, cols]).astype(bf16)
            first_grad = first_grad + dot_nt(up_grad, up[:, cols])
            up_bias_grads.append(column_sum(up_grad))
            up_new = dot_tn(first_low, up_grad)
            down_new = dot_tn(branch_grad, activated[:, cols])
            if number == 0:
                up_total[:, cols] = up_new
                down_total_t[:, cols] = down_new
            else:
                up_total[:, cols] += up_new
                down_total_t[:, cols] += down_new
        residual_grad = normal_back(first_grad, first_normal, first_scale, first_gain)
        attn_grad = residual_grad.astype(bf16)
        attn_block[here, :] = attn_grad
        back_a[:, at] = dot_nt(proj[rows_a, :], attn_grad).astype(bf16)
        back_b[:, at] = dot_nt(proj[rows_b, :], attn_grad).astype(bf16)
        new_a, new_b = dot(heads_a, attn_grad), dot(heads_b, attn_grad)
        if number == 0:
            proj_total[rows_a, :] = new_a
            proj_total[rows_b, :] = new_b
        else:
            proj_total[rows_a, :] += new_a
            proj_total[rows_b, :] += new_b
        new = [
            column_sum(attn_grad),
            column_sum(first_grad * first_normal),
            column_sum(first_grad),
            column_sum(branch_grad),
            column_sum(out_grad * second_normal),
            column_sum(out_grad),
        ] + up_bias_grads
        sums = new if sums is None else [a + b for a, b in zip(sums, new)]
    vector_rows = jnp.concatenate(sums + [jnp.zeros((6, D), f32)], axis=0)
    for pair in range(4):
        down_rows = jnp.transpose(down_total_t[:, D * pair : D * pair + D])
        for inner_step in range(2):
            step = 2 * pair + inner_step
            rows = slice(48 * step, 48 * step + 48)
            stacked = jnp.concatenate(
                [proj_total[rows, :]]
                + [up_total[rows, D * block : D * block + D] for block in range(4)]
                + [down_rows[192 * inner_step : 192 * inner_step + 192], vector_rows],
                axis=0,
            ).astype(bf16)
            packed_rows = slice(256 * step, 256 * step + 256)
            packed_keep[packed_rows, :] = dot(choice_t[core], stacked).astype(bf16)
            packed_send[packed_rows, :] = dot(choice_t[1 - core], stacked).astype(bf16)


def finish(
    place, joint, joint_core, joint_near, joint_across, half, mine_tokens, got,
    tokens_grad, qkv, q_bias, v_bias, proj, proj_bias, first_gain, first_shift, up, up_bias, down, down_bias, second_gain, second_shift,
):
    rank = place[2]
    here = place[0] == place[1]
    mine = jnp.where(here, joint[...], joint_near[...])
    theirs = jnp.where(here, joint_core[...], joint_across[...])
    total = jnp.stack([jnp.where(place[1] == 0, mine, theirs), jnp.where(place[1] == 0, theirs, mine)])
    columns = []
    for first, tail_row, tail_lane in ((0, 18, 0), (6, 18, 64), (12, 24, 0)):
        for side in range(2):
            columns.append(total[side, first : first + 6, :])
            columns.append(total[side, tail_row : tail_row + 6, tail_lane : tail_lane + 64])
    qkv[...] = jnp.concatenate(columns, axis=1)
    tokens_grad[place[0]] = mine_tokens[...]
    tokens_grad[1 - place[0]] = got[0:HALF, :]
    low, high = half[...].astype(f32), got[HALF:, :].astype(f32)
    first = place[0] == 0
    rest = jnp.concatenate([jnp.where(first, low, high), jnp.where(first, high, low)], axis=0)
    proj[...] = rest[0:6]
    up[...] = jnp.concatenate([rest[6 + 6 * block : 12 + 6 * block] for block in range(4)], axis=1)
    down[...] = rest[30:54]
    biases = [
        jnp.concatenate([total[0, row : row + 1], total[0, end : end + 1, 64:], total[1, row : row + 1], total[1, end : end + 1, 64:]], axis=1)
        for row, end in ((30, 24), (31, 25))
    ]
    vectors = jnp.concatenate(biases + [rest[54:60]], axis=0)
    vectors = pltpu.roll(vectors, lax.rem(D - ROWS * rank, D), 1)
    for at, out in enumerate((q_bias, v_bias, proj_bias, first_gain, first_shift, down_bias, second_gain, second_shift)):
        out[...] = vectors[at, 0:ROWS]
    long = jnp.concatenate([rest[60 + at : 61 + at] for at in range(4)], axis=1)
    long = pltpu.roll(jnp.concatenate([long] * 8, axis=0), lax.rem(FF - 24 * rank, FF), 1)
    up_bias[...] = long[0, 0:24]


def swap_core(value):
    return lax.ppermute(value, "c", SWAP)


def from_along(value, axis, step):
    return lax.ppermute(value, axis, tuple(((at + step) % 4, at) for at in range(4)))


def swap_ctx(value):
    return lax.ppermute(value, "zl", SWAP)


def spread_out(vector, rank):
    size = vector.shape[0]
    return lax.dynamic_update_slice(jnp.zeros((size * RANKS,), bf16), vector, (size * rank,))


def pack_joint(qkv_weight, query_bias, value_bias, rank):
    query_all, value_all = spread_out(query_bias, rank), spread_out(value_bias, rank)
    pieces = []
    for core in range(2):
        q, k, v = (qkv_weight[:, D * at + PART * core : D * at + PART * core + PART] for at in range(3))
        q_bias, v_bias = (part[PART * core : PART * core + PART] for part in (query_all, value_all))
        ends = jnp.concatenate([q_bias[None, 128:], v_bias[None, 128:], jnp.zeros((4, 64), bf16)], axis=0)
        pieces.append(
            jnp.concatenate(
                [
                    q[:, :128],
                    k[:, :128],
                    v[:, :128],
                    jnp.concatenate([q[:, 128:], k[:, 128:]], axis=1),
                    jnp.concatenate([v[:, 128:], ends], axis=1),
                    q_bias[None, :128],
                    v_bias[None, :128],
                ],
                axis=0,
            )
        )
    return jnp.stack(pieces)


def pack_rest(proj_weight, up_weight, down_weight, vectors, up_bias, rank):
    return jnp.concatenate(
        [proj_weight]
        + [up_weight[:, D * block : D * block + D] for block in range(4)]
        + [down_weight]
        + [spread_out(vector, rank)[None] for vector in vectors]
        + [spread_out(up_bias, rank).reshape(4, D)],
        axis=0,
    )


def spans_of(ids):
    first, last = ids[0, 0::TILE], ids[0, TILE - 1 :: TILE]
    low = jnp.sum(ids < first[:, None], axis=1, dtype=jnp.int32) // 128
    high = (jnp.sum(ids <= last[:, None], axis=1, dtype=jnp.int32) + 127) // 128
    needed = high - low
    width = jnp.where(needed <= WIDTHS[0], WIDTHS[0], jnp.where(needed <= WIDTHS[1], WIDTHS[1], WIDTHS[2]))
    return jnp.stack([jnp.minimum(low, 8 - width), width])


def local(
    tokens, segment_ids, out_grad, qkv_weight, query_bias, value_bias, proj_weight, proj_bias, first_gain, first_shift,
    up_weight, up_bias, down_weight, down_bias, second_gain, second_shift,
):
    x, y, zh, core, near = (lax.axis_index(name) for name in ALL)
    rank = ((x * 4 + y) * 2 + zh) * 2 + core
    groups = RANKS // 2
    place = jnp.stack([near, core, rank, x, y, zh]).astype(jnp.int32)
    take = functools.partial(lax.dynamic_index_in_dim, axis=0, keepdims=False)

    piece = pack_joint(qkv_weight, query_bias, value_bias, rank)
    piece = lax.dynamic_slice_in_dim(piece, 16 * near, 16, axis=1)
    sent = jnp.broadcast_to(piece[None, :, None], (groups, 2, 2, 16, 128)).reshape(4 * groups, 16, 128)
    joint_packed = lax.all_to_all(sent, ALL, 0, 0, tiled=True).reshape(groups * 64, 128)

    own = take(tokens, near)
    received = swap_ctx(take(tokens, 1 - near))
    ids_own = take(segment_ids, near)
    ids_received = swap_ctx(take(segment_ids, 1 - near))
    ids = jnp.where(near == 0, jnp.concatenate([ids_own, ids_received]), jnp.concatenate([ids_received, ids_own]))[None]
    own_other, received_other = swap_core(own), swap_core(received)
    ids, received_other = lax.optimization_barrier((ids, received_other))
    ids_other = swap_core(ids)
    grad_own = take(out_grad, near)
    grad_sent = take(out_grad, 1 - near)

    piece = pack_rest(
        proj_weight, up_weight, down_weight,
        (proj_bias, first_gain, first_shift, down_bias, second_gain, second_shift), up_bias, rank,
    )
    piece = lax.dynamic_slice_in_dim(piece, 32 * near, 32, axis=0)
    sent = jnp.broadcast_to(piece[None], (2 * groups, 32, D))
    sent, grad_sent, joint_packed, received, received_other, own_other, ids_other = lax.optimization_barrier(
        (sent, grad_sent, joint_packed, received, received_other, own_other, ids_other)
    )
    packed_a = lax.all_to_all(sent, ("x", "y", "zh", "zl"), 0, 0, tiled=True).reshape(groups * 64, D)
    spans, spans_other = spans_of(ids), spans_of(ids_other)
    ids_other, ids = ids_other.astype(f32), ids.astype(f32)

    choice = joint_choice()
    weight, weight_t, bias, bias_t = call(
        unpack_joint, 2, [((D, 768), bf16), ((768, D), bf16), ((8, 256), f32), ((256, 128), f32)], name="unpack"
    )(joint_packed, jnp.asarray(choice, bf16))

    grad_received = swap_ctx(grad_sent)
    tiles = SEQ // TILE
    saved = [((SEQ, 256), bf16), ((SEQ, 256), bf16), ((PART, SEQ), bf16), ((PART, SEQ), bf16), ((8, SEQ), f32)]
    *all_kept, probs, probs_other = call(
        attend,
        10,
        saved + saved + [((tiles, tiles, 6, TILE, TILE), bf16)] * 2,
        scratch=[
            pltpu.VMEM((PART, SEQ), bf16), pltpu.VMEM((SEQ, 256), bf16), pltpu.VMEM((PART + 16, SEQ), bf16),
            pltpu.VMEM((SEQ, 128), f32), pltpu.VMEM((2, 6, SEQ, TILE), bf16), pltpu.SemaphoreType.DMA((2, tiles)),
        ],
        scalars=3,
        flops=16 * 10**9,
        name="attend",
        far_outs=2,
    )(
        place, spans, spans_other, own, received, own_other, received_other, weight, weight_t, bias, bias_t, ids, ids_other,
    )
    kept, kept_other = all_kept[:5], all_kept[5:]
    mixed_a, mixed_other, packed_a, grad_received = lax.optimization_barrier((kept[3], kept_other[3], packed_a, grad_received))
    mixed_b, packed_b = swap_core(mixed_other), swap_core(packed_a)

    out_own, out_received, attn_own, attn_received, back_a, back_b, packed_keep, packed_send = call(
        feed_forward,
        10,
        [((HALF, D), bf16)] * 4 + [((PART, SEQ), bf16)] * 2 + [((2048, D), bf16)] * 2,
        scratch=[
            pltpu.VMEM((D, D), bf16), pltpu.VMEM((D, FF), bf16), pltpu.VMEM((FF, D), bf16), pltpu.VMEM((D, FF), f32),
            pltpu.VMEM((D, FF), f32), pltpu.VMEM((D, D), f32), pltpu.VMEM((FFN_ROWS, FF), bf16),
            pltpu.VMEM((FFN_ROWS, FF), f32),
        ],
        scalars=1,
        flops=10 * 10**9,
        name="feed_forward",
        limit=52,
        near=(5, 6, 7),
    )(
        place, own, received, grad_own, grad_received, mixed_a, keep_near(mixed_b),
        jnp.asarray(rest_choice(), bf16), jnp.asarray(rest_choice().transpose(0, 2, 1), bf16), keep_near(packed_a),
        keep_near(packed_b),
    )

    back_other = swap_core(back_b)
    packed_got = swap_core(packed_send)
    rest_sum = (packed_keep.astype(f32) + packed_got.astype(f32)).astype(bf16).reshape(2 * groups, 32, D)
    rest_sum, back_other, back_a, out_received = lax.optimization_barrier((rest_sum, back_other, back_a, out_received))
    out_back = swap_ctx(out_received)
    rest_all = lax.all_to_all(rest_sum, ("x", "y", "zh", "zl"), 0, 0, tiled=True)

    back_scratch = [
        pltpu.VMEM((PART, SEQ), f32), pltpu.VMEM((SEQ, 256), bf16), pltpu.VMEM((PART, SEQ), bf16),
        pltpu.VMEM((96, SEQ), bf16), pltpu.VMEM((2, 6, TILE, SEQ), bf16), pltpu.SemaphoreType.DMA((2, tiles)),
    ]
    rows = ((SEQ, 256), bf16)
    partial, partial_other, joint_sent = call(
        attend_back,
        20,
        [((SEQ, D), bf16), ((SEQ, D), bf16), ((2048, 128), bf16)],
        scratch=[pltpu.VMEM(*rows)] * 3 + [pltpu.VMEM((SEQ, D), bf16), pltpu.VMEM((D, 768), f32)] + back_scratch,
        scalars=3,
        flops=40 * 10**9,
        name="attend_back",
        limit=58,
        near=(1,),
        far_ins=2,
    )(
        place, spans, spans_other, own, received, weight_t, *kept, back_a, *kept_other, keep_near(back_other), own_other, received_other,
        jnp.asarray(choice.T, bf16), probs, probs_other,
    )
    joint_sent, partial_other, rest_all, out_back = lax.optimization_barrier((joint_sent, partial_other, rest_all, out_back))

    partial_got = swap_core(partial_other)
    rest_half = jnp.sum(rest_all.astype(f32), axis=0).astype(bf16)
    whole = partial.astype(f32) + partial_got.astype(f32)
    mine = lax.dynamic_slice_in_dim(whole, HALF * near, HALF, axis=0) + attn_own.astype(f32)
    theirs = lax.dynamic_slice_in_dim(whole, HALF * (1 - near), HALF, axis=0) + attn_received.astype(f32)
    mine, theirs = mine.astype(bf16), theirs.astype(bf16)
    got = swap_ctx(jnp.concatenate([theirs, rest_half]))

    joint_all = lax.all_to_all(joint_sent.reshape(RANKS, 32, 128), ("x", "y", "zh", "zl"), 0, 0, tiled=True)
    joint_sum = jnp.sum(joint_all.astype(f32), axis=0)
    joint_parts = [
        joint_sum,
        swap_core(joint_sum),
        swap_ctx(joint_sum),
        lax.ppermute(joint_sum, ("c", "zl"), ((0, 3), (3, 0), (1, 2), (2, 1))),
    ]
    vector = ((ROWS,), f32)
    tokens_grad, *grads = call(
        finish,
        7,
        [
            ((2, HALF, D), bf16), ((ROWS, 3 * D), f32), vector, vector, ((ROWS, D), f32), vector, vector, vector, ((ROWS, FF), f32),
            ((24,), f32), ((24, D), f32), vector, vector, vector,
        ],
        scalars=1,
        name="finish",
        limit=16,
    )(place, *joint_parts, rest_half, mine, got)
    layer_out = jnp.where(near == 0, jnp.stack([out_own, out_back]), jnp.stack([out_back, out_own]))
    return (layer_out, tokens_grad, *grads)


def solution(mesh):
    grid = Mesh(mesh.devices.reshape(4, 4, 2, 2, 2), ALL)
    ranks = ("x", "y", "zh", "c")
    data, matrix, vector = P(ranks, "zl", None), P(ranks, None), P(ranks)
    in_specs = (
        data, P(ranks, "zl"), data, matrix, vector, vector, matrix, vector, vector, vector, matrix, vector, matrix,
        vector, vector, vector,
    )
    out_specs = (
        data, data, matrix, vector, vector, matrix, vector, vector, vector, matrix, vector, matrix, vector, vector,
        vector,
    )
    return jax.shard_map(local, mesh=grid, in_specs=in_specs, out_specs=out_specs, check_vma=False)
```

```python
import functools
import math

import jax
import jax.numpy as jnp
import numpy as np
from jax import lax
from jax.experimental import pallas as pl
from jax.experimental.pallas import tpu as pltpu
from jax.sharding import Mesh
from jax.sharding import PartitionSpec as P

D = 384
FF = 1536
SEQ = 1024
HALF = 512
PART = 192
RANKS = 64
ROWS = D // RANKS
SCALE = 1.0 / math.sqrt(32)
LOG2E = math.log2(math.e)
BOUND = 60.0
TILE = 256
FFN_ROWS = 512
WIDTHS = (3, 5, 8)

bf16 = jnp.bfloat16
f32 = jnp.float32
VMEM = pl.BlockSpec(memory_space=pltpu.VMEM)
SMEM = pl.BlockSpec(memory_space=pltpu.SMEM)
FAR = pl.BlockSpec(memory_space=pl.ANY)
SWAP = ((0, 1), (1, 0))
ALL = ("x", "y", "zh", "c", "zl")


def dot(left, right):
    return lax.dot_general(left, right, (((1,), (0,)), ((), ())), preferred_element_type=f32)


def dot_nt(left, right):
    return lax.dot_general(left, right, (((1,), (1,)), ((), ())), preferred_element_type=f32)


def dot_tn(left, right):
    return lax.dot_general(left, right, (((0,), (0,)), ((), ())), preferred_element_type=f32)


def joint_choice():
    choice = np.zeros((256, 256), np.float32)
    for rank in range(8):
        for block in range(5):
            for row in range(ROWS):
                choice[48 * block + ROWS * rank + row, 32 * rank + ROWS * block + row] = 1
        for place, row in ((240, 30), (241, 31), (242, 24), (243, 25)):
            choice[place, 32 * rank + row] = 1
    return choice


def rest_choice():
    choice = np.zeros((2, 448, 256), np.float32)
    for core in range(2):
        for at in range(4):
            rank = 2 * at + core
            for row in range(ROWS):
                for block in range(5):
                    choice[core, 48 * block + ROWS * rank + row, 64 * at + ROWS * block + row] = 1
            for row in range(24):
                choice[core, 240 + 24 * rank + row, 64 * at + 30 + row] = 1
            for row in range(10):
                choice[core, 432 + row, 64 * at + 54 + row] = 1
    return choice


def call(kernel, ins, outs, scratch=(), scalars=0, flops=0, name=None, far_ins=0, far_outs=0, limit=56, near=()):
    return pl.pallas_call(
        kernel,
        in_specs=[SMEM] * scalars + [VMEM] * (ins - far_ins) + [FAR] * far_ins,
        out_specs=[VMEM] * (len(outs) - far_outs) + [FAR] * far_outs,
        out_shape=[
            pltpu.VMEM(shape, dtype) if at in near else jax.ShapeDtypeStruct(shape, dtype)
            for at, (shape, dtype) in enumerate(outs)
        ],
        scratch_shapes=scratch,
        compiler_params=pltpu.CompilerParams(vmem_limit_bytes=limit * 2**20),
        cost_estimate=pl.CostEstimate(flops=flops, bytes_accessed=4 * 2**20, transcendentals=0),
        name=name,
    )


def keep_near(value):
    return pltpu.with_memory_space_constraint(value, pltpu.VMEM)


def unpack_joint(packed, choice, weight, weight_t, bias, bias_t):
    low_lanes = lax.broadcasted_iota(jnp.int32, (48, 128), 1) < 64
    total = jnp.zeros((16, 128), f32)
    for step in range(8):
        out = dot(choice[...], packed[256 * step : 256 * step + 256, :])
        rows = slice(48 * step, 48 * step + 48)
        mixed = out[144:192]
        weight[rows, 0:128] = out[0:48].astype(bf16)
        weight[rows, 256:384] = out[48:96].astype(bf16)
        weight[rows, 512:640] = out[96:144].astype(bf16)
        weight[rows, 128:256] = jnp.where(low_lanes, mixed, 0.0).astype(bf16)
        weight[rows, 384:512] = jnp.where(low_lanes, pltpu.roll(mixed, 64, 1), 0.0).astype(bf16)
        weight[rows, 640:768] = jnp.where(low_lanes, out[192:240], 0.0).astype(bf16)
        total = total + out[240:256]
    tail = jnp.where(low_lanes[:16], pltpu.roll(total, 64, 1), 0.0)
    both = jnp.concatenate([total[0:2], jnp.zeros((6, 128), f32)], axis=0)
    tails = jnp.concatenate([tail[2:4], jnp.zeros((6, 128), f32)], axis=0)
    rows = jnp.concatenate([both, tails], axis=1)
    bias[...] = rows
    bias_t[...] = jnp.transpose(jnp.concatenate([rows, jnp.zeros((120, 256), f32)], axis=0))
    weight_t[...] = jnp.transpose(weight[...].astype(f32)).astype(bf16)


def padded_head(matrix, head, lanes, extra=None):
    parts = []
    if head:
        parts.append(jnp.zeros((32 * head, lanes), bf16))
    parts.append(matrix)
    if extra is None:
        parts.append(jnp.zeros((224 - 32 * head, lanes), bf16))
    else:
        if head < 5:
            parts.append(jnp.zeros((160 - 32 * head, lanes), bf16))
        parts.append(extra)
        parts.append(jnp.zeros((48, lanes), bf16))
    return jnp.concatenate(parts, axis=0)


def id_columns(id_row):
    return jnp.transpose(jnp.broadcast_to(id_row, (128, SEQ)))


def met(spans, one, other):
    def reached(tile, by):
        return (2 * tile + 1 >= spans[0, by]) & (2 * tile < spans[0, by] + spans[1, by])

    return reached(one, other) | reached(other, one)


def attend(
    place, spans_a, spans_b, own_a, received_a, own_b, received_b, weight, weight_t, bias, bias_t, id_row_a, id_row_b,
    q_rows_a, v_rows_a, k_t_a, mixed_t_a, inverse_a, q_rows_b, v_rows_b, k_t_b, mixed_t_b, inverse_b, probs_a, probs_b, *scratch,
):
    shared = (weight, weight_t, bias, bias_t)
    left = attend_to(
        place, spans_b, own_b, received_b, *shared, id_row_b, q_rows_b, v_rows_b, k_t_b, mixed_t_b, inverse_b, probs_b, None,
        *scratch,
    )
    left = attend_to(
        place, spans_a, own_a, received_a, *shared, id_row_a, q_rows_a, v_rows_a, k_t_a, mixed_t_a, inverse_a, probs_a, left,
        *scratch,
    )
    left()


def attend_to(
    place, spans, own, received, weight, weight_t, bias, bias_t, id_row,
    q_rows, v_rows, k_t, mixed_t, inverse, probs_far, before, q_t, k_rows, v_t, ids_t, probs_t, sems,
):
    lane = lax.broadcasted_iota(jnp.int32, (HALF, 256), 1) < PART
    for half, block in ((place[0], own), (1 - place[0], received)):
        at = pl.ds(pl.multiple_of(half * HALF, HALF), HALF)
        tokens = block[...]
        flat = dot(tokens, weight[...])
        q_rows[at, :] = ((flat[:, 0:256] + bias[0:1, :]) * (SCALE * LOG2E)).astype(bf16)
        k_rows[at, :] = flat[:, 256:512].astype(bf16)
        v_rows[at, :] = jnp.where(lane, flat[:, 512:768] + bias[1:2, :], 1.0).astype(bf16)
        q_t[:, at] = ((dot_nt(weight_t[0:PART, :], tokens) + bias_t[0:PART, 0:1]) * (SCALE * LOG2E)).astype(bf16)
        k_t[:, at] = dot_nt(weight_t[256 : 256 + PART, :], tokens).astype(bf16)
        v_t[0:PART, at] = (dot_nt(weight_t[512 : 512 + PART, :], tokens) + bias_t[0:PART, 1:2]).astype(bf16)
    v_t[PART:, :] = jnp.ones((16, SEQ), bf16)
    ids_t[...] = id_columns(id_row[...])
    inverse[...] = jnp.ones_like(inverse)
    largest = jnp.zeros((), f32)
    for head in range(6):
        rows = slice(32 * head, 32 * head + 32)
        q_size = jnp.max(jnp.sum(jnp.square(q_t[rows, :].astype(f32)), axis=0, keepdims=True))
        k_size = jnp.max(jnp.sum(jnp.square(k_t[rows, :].astype(f32)), axis=0, keepdims=True))
        largest = jnp.maximum(largest, q_size * k_size)
    small = largest <= BOUND * BOUND

    def tile_of(tile, width, start, shift):
        at = pl.ds(pl.multiple_of(tile * TILE, TILE), TILE)
        keys = pl.ds(pl.multiple_of(start * 128, 128), 128 * width)
        slot = lax.rem(tile, 2)
        if width < 8:
            for block in range(8):

                @pl.when((block < start) | (block >= start + width))
                def _():
                    probs_t[slot, :, 128 * block : 128 * block + 128, :] = jnp.zeros((6, 128, TILE), bf16)

        same = jnp.concatenate([ids_t[keys, :]] * 2, axis=1) == id_row[:, at]
        keep = same.astype(f32).astype(bf16)

        def score(head):
            return dot(k_rows[keys, :], padded_head(q_t[32 * head : 32 * head + 32, at], head, TILE))

        ahead = [score(0)]
        for head in range(6):
            rows = slice(32 * head, 32 * head + 32)
            if head < 5:
                ahead.append(score(head + 1))
            scores = ahead[head]
            if shift:
                scores = jnp.where(same, scores, -1e30)
                probs = jnp.exp2(scores - jnp.max(scores, axis=0, keepdims=True)).astype(bf16)
            else:
                probs = jnp.exp2(scores).astype(bf16) * keep
            probs_t[slot, head, keys, :] = probs
            mixed = dot(jnp.concatenate([v_t[rows, keys], v_t[PART:, keys]], axis=0), probs)
            over = 1.0 / mixed[32:33]
            mixed_t[rows, at] = (mixed[0:32] * over).astype(bf16)
            inverse[head : head + 1, at] = over

    def copies(tile, go):
        slot = lax.rem(tile, 2)
        for other in range(SEQ // TILE):

            @pl.when(met(spans, tile, other))
            def _():
                copy = pltpu.make_async_copy(
                    probs_t.at[slot, :, TILE * other : TILE * other + TILE, :], probs_far.at[tile, other], sems.at[slot, other]
                )
                copy.start() if go else copy.wait()

    def step(tile, carried):
        @pl.when(tile >= 2)
        def _():
            copies(tile - 2, False)

        for width in WIDTHS:

            @pl.when(small & (spans[1, tile] == width))
            def _():
                tile_of(tile, width, spans[0, tile], False)

        @pl.when(jnp.logical_not(small))
        def _():
            tile_of(tile, 8, 0, True)

        copies(tile, True)
        return carried

    if before is not None:
        before()
    lax.fori_loop(0, SEQ // TILE, step, 0)

    def left():
        for tile in range(SEQ // TILE - 2, SEQ // TILE):
            copies(tile, False)

    return left


def three_terms(row):
    first = row.astype(bf16).astype(f32)
    second = (row - first).astype(bf16).astype(f32)
    third = row - first - second
    return jnp.concatenate([first, second, third, jnp.zeros((13, row.shape[1]), f32)], axis=0).astype(bf16)


def attend_back(
    place, spans_a, spans_b, own, received, weight_t,
    q_rows_a, v_rows_a, k_t_a, mixed_t_a, inverse_a, grad_a, q_rows_b, v_rows_b, k_t_b, mixed_t_b, inverse_b, grad_b,
    own_b, received_b, choice, probs_a, probs_b, tokens_a, tokens_b, packed, q_grad, k_grad, v_grad, x_rows, all_totals, *scratch,
):
    back_of(
        spans_a, weight_t, q_rows_a, v_rows_a, k_t_a, mixed_t_a, inverse_a, grad_a, probs_a, tokens_a, q_grad, k_grad, v_grad,
        *scratch,
    )
    totals, first_bias = joint_totals(place, own, received, x_rows, q_grad, k_grad, v_grad)
    for at, part in enumerate(totals):
        all_totals[:, 256 * at : 256 * at + 256] = part
    back_of(
        spans_b, weight_t, q_rows_b, v_rows_b, k_t_b, mixed_t_b, inverse_b, grad_b, probs_b, tokens_b, q_grad, k_grad, v_grad,
        *scratch,
    )
    totals, bias_rows = joint_totals(place, own_b, received_b, x_rows, q_grad, k_grad, v_grad)
    pack_totals([part + all_totals[:, 256 * at : 256 * at + 256] for at, part in enumerate(totals)], first_bias + bias_rows, choice, packed)


def back_of(
    spans, weight_t, q_rows, v_rows, k_t, mixed_t, inverse, mixed_grad_t, probs_far, tokens_grad, q_grad, k_grad, v_grad,
    q_grad_t, grad_rows, grad_t, extra_rows, probs_t, sems,
):
    def copies(tile, go):
        slot = lax.rem(tile, 2)
        for other in range(SEQ // TILE):

            @pl.when(met(spans, tile, other))
            def _():
                copy = pltpu.make_async_copy(
                    probs_far.at[other, tile], probs_t.at[slot, :, :, TILE * other : TILE * other + TILE], sems.at[slot, other]
                )
                copy.start() if go else copy.wait()

    copies(jnp.int32(0), True)
    scaled = []
    for head in range(6):
        rows = slice(32 * head, 32 * head + 32)
        part = mixed_grad_t[rows, :].astype(f32) * inverse[head : head + 1, :]
        delta = jnp.sum(part * mixed_t[rows, :].astype(f32), axis=0, keepdims=True)
        extra_rows[16 * head : 16 * head + 16, :] = three_terms(-delta)
        grad_t[rows, :] = part.astype(bf16)
        scaled.append(part)
    grad_rows[:, 0:PART] = jnp.transpose(jnp.concatenate(scaled, axis=0)).astype(bf16)
    grad_rows[:, PART:] = jnp.zeros((SEQ, 256 - PART), bf16)
    q_grad_t[...] = jnp.zeros_like(q_grad_t)

    def tile_of(tile, width, start):
        at = pl.ds(pl.multiple_of(tile * TILE, TILE), TILE)
        queries = pl.ds(pl.multiple_of(start * 128, 128), 128 * width)
        lane = lax.broadcasted_iota(jnp.int32, (128 * width, 256), 1)
        key_total = jnp.zeros((TILE, 256), f32)
        value_total = jnp.zeros((TILE, 256), f32)

        def spread(head):
            part = padded_head(
                grad_t[32 * head : 32 * head + 32, queries], head, 128 * width, extra_rows[16 * head : 16 * head + 16, queries]
            )
            return dot(v_rows[at, :], part)

        ahead = [spread(0)]
        for head in range(6):
            rows = slice(32 * head, 32 * head + 32)
            inside = (lane >= 32 * head) & (lane < 32 * head + 32)
            if head < 5:
                ahead.append(spread(head + 1))
            probs = probs_t[lax.rem(tile, 2), head, :, queries]
            scores_grad = probs * ahead[head].astype(bf16)
            one, other = q_rows[queries, :], grad_rows[queries, :]
            key_total += dot(scores_grad, jnp.where(inside, one, jnp.zeros_like(one)))
            value_total += dot(probs, jnp.where(inside, other, jnp.zeros_like(other)))
            q_grad_t[rows, queries] += dot(k_t[rows, at], scores_grad)
        k_grad[at, :] = (key_total * (1.0 / LOG2E)).astype(bf16)
        v_grad[at, :] = value_total.astype(bf16)

    def step(tile, carried):
        @pl.when(tile + 1 < SEQ // TILE)
        def _():
            copies(tile + 1, True)

        copies(tile, False)
        for width in WIDTHS:

            @pl.when(spans[1, tile] == width)
            def _():
                tile_of(tile, width, spans[0, tile])

        return carried

    lax.fori_loop(0, SEQ // TILE, step, 0)
    q_grad[:, 0:PART] = jnp.transpose(q_grad_t[...] * SCALE).astype(bf16)
    q_grad[:, PART:] = jnp.zeros((SEQ, 256 - PART), bf16)
    tokens_grad[...] = (
        dot(q_grad[:, 0:PART], weight_t[0:PART, :])
        + dot(k_grad[:, 0:PART], weight_t[256 : 256 + PART, :])
        + dot(v_grad[:, 0:PART], weight_t[512 : 512 + PART, :])
    ).astype(bf16)


def joint_totals(place, own, received, x_rows, q_grad, k_grad, v_grad):
    for half, block in ((place[0], own), (1 - place[0], received)):
        x_rows[pl.ds(pl.multiple_of(half * HALF, HALF), HALF), :] = block[...]
    totals = [dot_tn(x_rows[...], part[...]) for part in (q_grad, k_grad, v_grad)]
    bias_rows = jnp.concatenate(
        [jnp.sum(part[...].astype(f32), axis=0, keepdims=True) for part in (q_grad, v_grad)] + [jnp.zeros((6, 256), f32)],
        axis=0,
    )
    return totals, bias_rows


def pack_totals(totals, bias_rows, choice, packed):
    q_all, k_all, v_all = totals
    low_lanes = lax.broadcasted_iota(jnp.int32, (D, 128), 1) < 64
    fourth = jnp.where(low_lanes, q_all[:, 128:], pltpu.roll(k_all[:, 128:], 64, 1))
    fifth = jnp.where(low_lanes, v_all[:, 128:], 0.0)
    ends = jnp.where(low_lanes[:8], 0.0, pltpu.roll(bias_rows[:, 128:], 64, 1))
    biases = jnp.concatenate([bias_rows[0:2, 0:128], ends[0:2], jnp.zeros((12, 128), f32)], axis=0)
    for step_at in range(8):
        rows = slice(48 * step_at, 48 * step_at + 48)
        stacked = jnp.concatenate(
            [q_all[rows, 0:128], k_all[rows, 0:128], v_all[rows, 0:128], fourth[rows], fifth[rows], biases], axis=0
        ).astype(bf16)
        packed[256 * step_at : 256 * step_at + 256, :] = dot(choice[...], stacked).astype(bf16)


def normal_parts(values):
    mean = jnp.mean(values, axis=-1, keepdims=True)
    centered = values - mean
    scale = lax.rsqrt(jnp.mean(centered * centered, axis=-1, keepdims=True) + 1e-05)
    return centered * scale, scale


def normal_back(cotangent, normal, scale, gain):
    weighted = cotangent * gain
    mean = jnp.mean(weighted, axis=-1, keepdims=True)
    along = jnp.mean(weighted * normal, axis=-1, keepdims=True)
    return scale * (weighted - mean - normal * along)


def column_sum(matrix):
    return jnp.sum(matrix.astype(f32), axis=0, keepdims=True)


def feed_forward(
    place, own, received, own_grad, received_grad, mixed_a, mixed_b, choice, choice_t,
    packed_a, packed_b,
    out_own, out_received, attn_own, attn_received, back_a, back_b, packed_keep, packed_send,
    proj, up, down, up_total, down_total_t, proj_total, activated, slope,
):
    core, near = place[1], place[0]
    vectors = jnp.zeros((16, D), f32)
    for step in range(8):
        rows = slice(256 * step, 256 * step + 256)
        out = dot(choice[core], packed_a[rows, :]) + dot(choice[1 - core], packed_b[rows, :])
        proj[48 * step : 48 * step + 48, :] = out[0:48].astype(bf16)
        for block in range(4):
            up[48 * step : 48 * step + 48, D * block : D * block + D] = out[48 + 48 * block : 96 + 48 * block].astype(bf16)
        down[192 * step : 192 * step + 192, :] = out[240:432].astype(bf16)
        vectors = vectors + out[432:448]
    proj_bias, first_gain, first_shift, down_bias, second_gain, second_shift = (vectors[i : i + 1] for i in range(6))
    up_bias = jnp.concatenate([vectors[i : i + 1] for i in range(6, 10)], axis=1)
    rows_a = pl.ds(pl.multiple_of(core * PART, PART), PART)
    rows_b = pl.ds(pl.multiple_of((1 - core) * PART, PART), PART)
    sums = None
    blocks = ((near, own, own_grad, out_own, attn_own), (1 - near, received, received_grad, out_received, attn_received))
    for number in range(SEQ // FFN_ROWS):
        half, block, grad_block, out_block, attn_block = blocks[number * FFN_ROWS // HALF]
        inside = number * FFN_ROWS % HALF
        here = slice(inside, inside + FFN_ROWS)
        at = pl.ds(pl.multiple_of(half * HALF + inside, FFN_ROWS), FFN_ROWS)
        heads_a, heads_b = mixed_a[:, at], mixed_b[:, at]
        residual = block[here, :].astype(f32) + (dot_tn(heads_a, proj[rows_a, :]) + dot_tn(heads_b, proj[rows_b, :]) + proj_bias)
        first_normal, first_scale = normal_parts(residual)
        first_norm = first_normal * first_gain + first_shift
        first_low = first_norm.astype(bf16)
        for col in range(4):
            cols = slice(D * col, D * col + D)
            hidden = dot(first_low, up[:, cols]) + up_bias[:, cols]
            bell = jnp.exp2(hidden * hidden * (-0.5 * LOG2E))
            inner = 1.0 / (1.0 + jnp.abs(hidden) * (0.3275911 / math.sqrt(2)))
            series = inner * (0.127414796 + inner * (-0.142248368 + inner * (0.7107068705 + inner * (-0.7265760135 + inner * 0.5307027145))))
            tail = series * bell
            below = jnp.where(hidden >= 0.0, 1.0 - tail, tail)
            activated[:, cols] = (hidden * below).astype(bf16)
            slope[:, cols] = below + hidden * bell * (1.0 / math.sqrt(2 * math.pi))
        second_sum = first_norm + (dot(activated[...], down[...]) + down_bias)
        second_normal, second_scale = normal_parts(second_sum)
        out_block[here, :] = (second_normal * second_gain + second_shift).astype(bf16)
        out_grad = grad_block[here, :].astype(f32)
        second_grad = normal_back(out_grad, second_normal, second_scale, second_gain)
        branch_grad = second_grad.astype(bf16)
        first_grad = second_grad
        up_bias_grads = []
        for col in range(4):
            cols = slice(D * col, D * col + D)
            up_grad = (dot_nt(branch_grad, down[cols, :]) * slope[:, cols]).astype(bf16)
            first_grad = first_grad + dot_nt(up_grad, up[:, cols])
            up_bias_grads.append(column_sum(up_grad))
            up_new = dot_tn(first_low, up_grad)
            down_new = dot_tn(branch_grad, activated[:, cols])
            if number == 0:
                up_total[:, cols] = up_new
                down_total_t[:, cols] = down_new
            else:
                up_total[:, cols] += up_new
                down_total_t[:, cols] += down_new
        residual_grad = normal_back(first_grad, first_normal, first_scale, first_gain)
        attn_grad = residual_grad.astype(bf16)
        attn_block[here, :] = attn_grad
        back_a[:, at] = dot_nt(proj[rows_a, :], attn_grad).astype(bf16)
        back_b[:, at] = dot_nt(proj[rows_b, :], attn_grad).astype(bf16)
        new_a, new_b = dot(heads_a, attn_grad), dot(heads_b, attn_grad)
        if number == 0:
            proj_total[rows_a, :] = new_a
            proj_total[rows_b, :] = new_b
        else:
            proj_total[rows_a, :] += new_a
            proj_total[rows_b, :] += new_b
        new = [
            column_sum(attn_grad),
            column_sum(first_grad * first_normal),
            column_sum(first_grad),
            column_sum(branch_grad),
            column_sum(out_grad * second_normal),
            column_sum(out_grad),
        ] + up_bias_grads
        sums = new if sums is None else [a + b for a, b in zip(sums, new)]
    vector_rows = jnp.concatenate(sums + [jnp.zeros((6, D), f32)], axis=0)
    for pair in range(4):
        down_rows = jnp.transpose(down_total_t[:, D * pair : D * pair + D])
        for inner_step in range(2):
            step = 2 * pair + inner_step
            rows = slice(48 * step, 48 * step + 48)
            stacked = jnp.concatenate(
                [proj_total[rows, :]]
                + [up_total[rows, D * block : D * block + D] for block in range(4)]
                + [down_rows[192 * inner_step : 192 * inner_step + 192], vector_rows],
                axis=0,
            ).astype(bf16)
            packed_rows = slice(256 * step, 256 * step + 256)
            packed_keep[packed_rows, :] = dot(choice_t[core], stacked).astype(bf16)
            packed_send[packed_rows, :] = dot(choice_t[1 - core], stacked).astype(bf16)


def finish(
    place, joint, joint_core, joint_near, joint_across, half, mine_tokens, got,
    tokens_grad, qkv, q_bias, v_bias, proj, proj_bias, first_gain, first_shift, up, up_bias, down, down_bias, second_gain, second_shift,
):
    rank = place[2]
    here = place[0] == place[1]
    mine = jnp.where(here, joint[...], joint_near[...])
    theirs = jnp.where(here, joint_core[...], joint_across[...])
    total = jnp.stack([jnp.where(place[1] == 0, mine, theirs), jnp.where(place[1] == 0, theirs, mine)])
    columns = []
    for first, tail_row, tail_lane in ((0, 18, 0), (6, 18, 64), (12, 24, 0)):
        for side in range(2):
            columns.append(total[side, first : first + 6, :])
            columns.append(total[side, tail_row : tail_row + 6, tail_lane : tail_lane + 64])
    qkv[...] = jnp.concatenate(columns, axis=1)
    tokens_grad[place[0]] = mine_tokens[...]
    tokens_grad[1 - place[0]] = got[0:HALF, :]
    low, high = half[...].astype(f32), got[HALF:, :].astype(f32)
    first = place[0] == 0
    rest = jnp.concatenate([jnp.where(first, low, high), jnp.where(first, high, low)], axis=0)
    proj[...] = rest[0:6]
    up[...] = jnp.concatenate([rest[6 + 6 * block : 12 + 6 * block] for block in range(4)], axis=1)
    down[...] = rest[30:54]
    biases = [
        jnp.concatenate([total[0, row : row + 1], total[0, end : end + 1, 64:], total[1, row : row + 1], total[1, end : end + 1, 64:]], axis=1)
        for row, end in ((30, 24), (31, 25))
    ]
    vectors = jnp.concatenate(biases + [rest[54:60]], axis=0)
    vectors = pltpu.roll(vectors, lax.rem(D - ROWS * rank, D), 1)
    for at, out in enumerate((q_bias, v_bias, proj_bias, first_gain, first_shift, down_bias, second_gain, second_shift)):
        out[...] = vectors[at, 0:ROWS]
    long = jnp.concatenate([rest[60 + at : 61 + at] for at in range(4)], axis=1)
    long = pltpu.roll(jnp.concatenate([long] * 8, axis=0), lax.rem(FF - 24 * rank, FF), 1)
    up_bias[...] = long[0, 0:24]


def swap_core(value):
    return lax.ppermute(value, "c", SWAP)


def from_along(value, axis, step):
    return lax.ppermute(value, axis, tuple(((at + step) % 4, at) for at in range(4)))


def swap_ctx(value):
    return lax.ppermute(value, "zl", SWAP)


def spread_out(vector, rank):
    size = vector.shape[0]
    return lax.dynamic_update_slice(jnp.zeros((size * RANKS,), bf16), vector, (size * rank,))


def pack_joint(qkv_weight, query_bias, value_bias, rank):
    query_all, value_all = spread_out(query_bias, rank), spread_out(value_bias, rank)
    pieces = []
    for core in range(2):
        q, k, v = (qkv_weight[:, D * at + PART * core : D * at + PART * core + PART] for at in range(3))
        q_bias, v_bias = (part[PART * core : PART * core + PART] for part in (query_all, value_all))
        ends = jnp.concatenate([q_bias[None, 128:], v_bias[None, 128:], jnp.zeros((4, 64), bf16)], axis=0)
        pieces.append(
            jnp.concatenate(
                [
                    q[:, :128],
                    k[:, :128],
                    v[:, :128],
                    jnp.concatenate([q[:, 128:], k[:, 128:]], axis=1),
                    jnp.concatenate([v[:, 128:], ends], axis=1),
                    q_bias[None, :128],
                    v_bias[None, :128],
                ],
                axis=0,
            )
        )
    return jnp.stack(pieces)


def pack_rest(proj_weight, up_weight, down_weight, vectors, up_bias, rank):
    return jnp.concatenate(
        [proj_weight]
        + [up_weight[:, D * block : D * block + D] for block in range(4)]
        + [down_weight]
        + [spread_out(vector, rank)[None] for vector in vectors]
        + [spread_out(up_bias, rank).reshape(4, D)],
        axis=0,
    )


def spans_of(ids):
    first, last = ids[0, 0::TILE], ids[0, TILE - 1 :: TILE]
    low = jnp.sum(ids < first[:, None], axis=1, dtype=jnp.int32) // 128
    high = (jnp.sum(ids <= last[:, None], axis=1, dtype=jnp.int32) + 127) // 128
    needed = high - low
    width = jnp.where(needed <= WIDTHS[0], WIDTHS[0], jnp.where(needed <= WIDTHS[1], WIDTHS[1], WIDTHS[2]))
    return jnp.stack([jnp.minimum(low, 8 - width), width])


def local(
    tokens, segment_ids, out_grad, qkv_weight, query_bias, value_bias, proj_weight, proj_bias, first_gain, first_shift,
    up_weight, up_bias, down_weight, down_bias, second_gain, second_shift,
):
    x, y, zh, core, near = (lax.axis_index(name) for name in ALL)
    rank = ((x * 4 + y) * 2 + zh) * 2 + core
    groups = RANKS // 2
    place = jnp.stack([near, core, rank, x, y, zh]).astype(jnp.int32)
    take = functools.partial(lax.dynamic_index_in_dim, axis=0, keepdims=False)

    piece = pack_joint(qkv_weight, query_bias, value_bias, rank)
    piece = lax.dynamic_slice_in_dim(piece, 16 * near, 16, axis=1)
    sent = jnp.broadcast_to(piece[None, :, None], (groups, 2, 2, 16, 128)).reshape(4 * groups, 16, 128)
    joint_packed = lax.all_to_all(sent, ALL, 0, 0, tiled=True).reshape(groups * 64, 128)

    own = take(tokens, near)
    received = swap_ctx(take(tokens, 1 - near))
    ids_own = take(segment_ids, near)
    ids_received = swap_ctx(take(segment_ids, 1 - near))
    ids = jnp.where(near == 0, jnp.concatenate([ids_own, ids_received]), jnp.concatenate([ids_received, ids_own]))[None]
    own_other, received_other = swap_core(own), swap_core(received)
    ids, received_other = lax.optimization_barrier((ids, received_other))
    ids_other = swap_core(ids)
    grad_own = take(out_grad, near)
    grad_sent = take(out_grad, 1 - near)

    piece = pack_rest(
        proj_weight, up_weight, down_weight,
        (proj_bias, first_gain, first_shift, down_bias, second_gain, second_shift), up_bias, rank,
    )
    piece = lax.dynamic_slice_in_dim(piece, 32 * near, 32, axis=0)
    sent = jnp.broadcast_to(piece[None], (2 * groups, 32, D))
    sent, grad_sent, joint_packed, received, received_other, own_other, ids_other = lax.optimization_barrier(
        (sent, grad_sent, joint_packed, received, received_other, own_other, ids_other)
    )
    packed_a = lax.all_to_all(sent, ("x", "y", "zh", "zl"), 0, 0, tiled=True).reshape(groups * 64, D)
    spans, spans_other = spans_of(ids), spans_of(ids_other)
    ids_other, ids = ids_other.astype(f32), ids.astype(f32)

    choice = joint_choice()
    weight, weight_t, bias, bias_t = call(
        unpack_joint, 2, [((D, 768), bf16), ((768, D), bf16), ((8, 256), f32), ((256, 128), f32)], name="unpack"
    )(joint_packed, jnp.asarray(choice, bf16))

    grad_received = swap_ctx(grad_sent)
    tiles = SEQ // TILE
    saved = [((SEQ, 256), bf16), ((SEQ, 256), bf16), ((PART, SEQ), bf16), ((PART, SEQ), bf16), ((8, SEQ), f32)]
    *all_kept, probs, probs_other = call(
        attend,
        10,
        saved + saved + [((tiles, tiles, 6, TILE, TILE), bf16)] * 2,
        scratch=[
            pltpu.VMEM((PART, SEQ), bf16), pltpu.VMEM((SEQ, 256), bf16), pltpu.VMEM((PART + 16, SEQ), bf16),
            pltpu.VMEM((SEQ, 128), f32), pltpu.VMEM((2, 6, SEQ, TILE), bf16), pltpu.SemaphoreType.DMA((2, tiles)),
        ],
        scalars=3,
        flops=16 * 10**9,
        name="attend",
        limit=58,
        far_outs=2,
    )(
        place, spans, spans_other, keep_near(own), keep_near(received), keep_near(own_other), keep_near(received_other),
        weight, weight_t, bias, bias_t, ids, ids_other,
    )
    kept, kept_other = all_kept[:5], all_kept[5:]
    mixed_a, mixed_other, packed_a, grad_received = lax.optimization_barrier((kept[3], kept_other[3], packed_a, grad_received))
    mixed_b, packed_b = swap_core(mixed_other), swap_core(packed_a)

    out_own, out_received, attn_own, attn_received, back_a, back_b, packed_keep, packed_send = call(
        feed_forward,
        10,
        [((HALF, D), bf16)] * 4 + [((PART, SEQ), bf16)] * 2 + [((2048, D), bf16)] * 2,
        scratch=[
            pltpu.VMEM((D, D), bf16), pltpu.VMEM((D, FF), bf16), pltpu.VMEM((FF, D), bf16), pltpu.VMEM((D, FF), f32),
            pltpu.VMEM((D, FF), f32), pltpu.VMEM((D, D), f32), pltpu.VMEM((FFN_ROWS, FF), bf16),
            pltpu.VMEM((FFN_ROWS, FF), f32),
        ],
        scalars=1,
        flops=10 * 10**9,
        name="feed_forward",
        limit=52,
        near=(5, 6, 7),
    )(
        place, own, received, grad_own, grad_received, mixed_a, keep_near(mixed_b),
        jnp.asarray(rest_choice(), bf16), jnp.asarray(rest_choice().transpose(0, 2, 1), bf16), keep_near(packed_a),
        keep_near(packed_b),
    )

    back_other = swap_core(back_b)
    packed_got = swap_core(packed_send)
    rest_sum = (packed_keep.astype(f32) + packed_got.astype(f32)).astype(bf16).reshape(2 * groups, 32, D)
    rest_sum, back_other, back_a, out_received = lax.optimization_barrier((rest_sum, back_other, back_a, out_received))
    out_back = swap_ctx(out_received)
    rest_all = lax.all_to_all(rest_sum, ("x", "y", "zh", "zl"), 0, 0, tiled=True)

    back_scratch = [
        pltpu.VMEM((PART, SEQ), f32), pltpu.VMEM((SEQ, 256), bf16), pltpu.VMEM((PART, SEQ), bf16),
        pltpu.VMEM((96, SEQ), bf16), pltpu.VMEM((2, 6, TILE, SEQ), bf16), pltpu.SemaphoreType.DMA((2, tiles)),
    ]
    rows = ((SEQ, 256), bf16)
    partial, partial_other, joint_sent = call(
        attend_back,
        20,
        [((SEQ, D), bf16), ((SEQ, D), bf16), ((2048, 128), bf16)],
        scratch=[pltpu.VMEM(*rows)] * 3 + [pltpu.VMEM((SEQ, D), bf16), pltpu.VMEM((D, 768), f32)] + back_scratch,
        scalars=3,
        flops=40 * 10**9,
        name="attend_back",
        limit=58,
        near=(1,),
        far_ins=2,
    )(
        place, spans, spans_other, own, received, weight_t, *kept, back_a, *kept_other, keep_near(back_other), own_other, received_other,
        jnp.asarray(choice.T, bf16), probs, probs_other,
    )
    joint_sent, partial_other, rest_all, out_back = lax.optimization_barrier((joint_sent, partial_other, rest_all, out_back))

    partial_got = swap_core(partial_other)
    rest_half = jnp.sum(rest_all.astype(f32), axis=0).astype(bf16)
    whole = partial.astype(f32) + partial_got.astype(f32)
    mine = lax.dynamic_slice_in_dim(whole, HALF * near, HALF, axis=0) + attn_own.astype(f32)
    theirs = lax.dynamic_slice_in_dim(whole, HALF * (1 - near), HALF, axis=0) + attn_received.astype(f32)
    mine, theirs = mine.astype(bf16), theirs.astype(bf16)
    got = swap_ctx(jnp.concatenate([theirs, rest_half]))

    joint_all = lax.all_to_all(joint_sent.reshape(RANKS, 32, 128), ("x", "y", "zh", "zl"), 0, 0, tiled=True)
    joint_sum = jnp.sum(joint_all.astype(f32), axis=0)
    joint_parts = [
        joint_sum,
        swap_core(joint_sum),
        swap_ctx(joint_sum),
        lax.ppermute(joint_sum, ("c", "zl"), ((0, 3), (3, 0), (1, 2), (2, 1))),
    ]
    vector = ((ROWS,), f32)
    tokens_grad, *grads = call(
        finish,
        7,
        [
            ((2, HALF, D), bf16), ((ROWS, 3 * D), f32), vector, vector, ((ROWS, D), f32), vector, vector, vector, ((ROWS, FF), f32),
            ((24,), f32), ((24, D), f32), vector, vector, vector,
        ],
        scalars=1,
        name="finish",
        limit=16,
    )(place, *joint_parts, rest_half, mine, got)
    layer_out = jnp.where(near == 0, jnp.stack([out_own, out_back]), jnp.stack([out_back, out_own]))
    return (layer_out, tokens_grad, *grads)


def solution(mesh):
    grid = Mesh(mesh.devices.reshape(4, 4, 2, 2, 2), ALL)
    ranks = ("x", "y", "zh", "c")
    data, matrix, vector = P(ranks, "zl", None), P(ranks, None), P(ranks)
    in_specs = (
        data, P(ranks, "zl"), data, matrix, vector, vector, matrix, vector, vector, vector, matrix, vector, matrix,
        vector, vector, vector,
    )
    out_specs = (
        data, data, matrix, vector, vector, matrix, vector, vector, vector, matrix, vector, matrix, vector, vector,
        vector,
    )
    return jax.shard_map(local, mesh=grid, in_specs=in_specs, out_specs=out_specs, check_vma=False)
```
